512 devices in a mesh: seq: 128 (over z, y, core), ch: 4 (over x).
Axes of the slice: x: 4, y: 8, z: 8, core: 2. Of those that a mesh axis runs over, the one named last changes fastest.
Arguments:
- gate: bfloat16 [16384, 8, 512], P('seq', 'ch'), may hold values from -6 to 6
- value: bfloat16 [16384, 8, 512], P('seq', 'ch'), may hold values from -6 to 6
- filt: bfloat16 [16384, 512], P('seq'), may hold values from -6 to 6
- cotangent: bfloat16 [16384, 8, 512], P('seq', 'ch'), may hold values from -6 to 6
Outputs:
- out: bfloat16 [16384, 8, 512], P('seq', 'ch')
- gate_grad: bfloat16 [16384, 8, 512], P('seq', 'ch')
- value_grad: bfloat16 [16384, 8, 512], P('seq', 'ch')
- filt_grad: bfloat16 [16384, 512], P('seq', 'ch')
The draws below stay inside these ranges and needn't reach their ends.
All inputs are finite; a program needn't handle non-finite values.
Results may differ from the reference program's by a relative error of at most 0.0011.
Values sent between devices are 32-bit elements; how exact they have to be, the bound alone decides.
No kernel may reach another device: no remote copies, remote signals or barrier semaphores. Data moves between devices by JAX's collectives and lax.ppermute only.
A program may use at most 64 MiB of HBM per device.

```python
import math
import jax
import jax.numpy as jnp
from jax import lax

F = 512
GROUP = 8
TOKENS = 16384


def spiked(entries, stream_key, source, target, blocks, factor):
    owner, partner = [(jnp.arange(entries.shape[dim]) // (entries.shape[dim] // blocks)).reshape([-1 if axis == dim else 1 for axis in range(entries.ndim)]) for dim in (source, target)]
    chosen = jax.random.permutation(stream_key, blocks)[partner]
    strong = (owner == chosen) | (owner == (partner + blocks // 2) % blocks)
    return jnp.where(strong, factor * entries, entries)


def levels(key, extent, split, smallest, high):
    factor_of = 1.0
    for position, shards_of in split:
        heights = jax.random.uniform(jax.random.fold_in(jax.random.fold_in(key, 6), position), (shards_of,), jnp.float32, smallest / len(split), high / len(split))
        factor_of = factor_of * jnp.repeat(jnp.exp(heights), extent[position] // shards_of).reshape((-1,) + (1,) * (len(extent) - 1 - position))
    return factor_of


def noise(key, dims, scale, limit, cuts=(), dtype=jnp.bfloat16):
    values = jax.random.normal(key, dims, jnp.float32) * scale
    if len(cuts) > 0:
        values = levels(key, dims, cuts, -0.22, 0.18) * values
    return jnp.clip(values, min=-limit, max=limit).astype(dtype)


def bell_draw_with(own_key, shape, spread, reach, cuts, heavy, kind=jnp.bfloat16):
    values = spread * jax.random.normal(own_key, shape, jnp.float32)
    if cuts:
        values = values * levels(own_key, shape, cuts, -0.22, 0.18)
    return jnp.clip(spiked(values, jax.random.fold_in(own_key, 3), *heavy), -reach, reach).astype(kind)


def setup_inputs(seed: int = 0) -> dict:
    seeds = jax.random.split(jax.random.key(seed), 5)
    return {
        "gate": noise(seeds[0], (TOKENS, GROUP, F), 1.0, 6.0, ((0, 128), (1, 4))),
        "value": noise(seeds[1], (TOKENS, GROUP, F), 1.0, 6.0, ((0, 128), (1, 4))),
        "filt": noise(seeds[2], (TOKENS, F), 1.0, 6.0, ((0, 128),)),
        "cotangent": bell_draw_with(seeds[3], (TOKENS, GROUP, F), 1.0, 6.0, ((0, 128), (1, 4)), (1, 2, 4, 2.0)),
    }


def reference(gate, value, filt, cotangent):
    length = TOKENS
    padded = 2 * length
    inv_root = 1.0 / math.sqrt(TOKENS)
    width = math.gcd(F, 64)
    count = F // width

    def split_wide(array):
        shaped = array.reshape(array.shape[:-1] + (count, width))
        return jnp.moveaxis(shaped, -2, 0)

    def one_block(pieces):
        gate_blk, value_blk, filt_blk, cot_blk = pieces
        gate_f = gate_blk.astype(jnp.float32)
        value_f = value_blk.astype(jnp.float32)
        cot_f = cot_blk.astype(jnp.float32)
        filt_f = filt_blk.astype(jnp.float32) * inv_root
        value_spec = jnp.fft.rfft(value_f, n=padded, axis=0)
        filt_spec = jnp.fft.rfft(filt_f, n=padded, axis=0)[:, None, :]
        conv = jnp.fft.irfft(value_spec * filt_spec, n=padded, axis=0)[:length]
        out_blk = (gate_f * conv).astype(jnp.bfloat16)
        gate_grad_blk = (cot_f * conv).astype(jnp.bfloat16)
        gated = cot_f * gate_f
        gated_spec = jnp.fft.rfft(gated, n=padded, axis=0)
        value_grad_blk = jnp.fft.irfft(jnp.conj(filt_spec) * gated_spec, n=padded, axis=0)[:length]
        filt_total = lax.optimization_barrier(jnp.sum(jnp.conj(value_spec) * gated_spec, axis=1))
        filt_grad_blk = jnp.fft.irfft(filt_total, n=padded, axis=0)[:length] * inv_root
        return (out_blk, gate_grad_blk, value_grad_blk.astype(jnp.bfloat16), filt_grad_blk.astype(jnp.bfloat16))
    results = lax.map(one_block, (split_wide(gate), split_wide(value), split_wide(filt), split_wide(cotangent)))

    def merge_wide(array):
        moved = jnp.moveaxis(array, 0, -2)
        return moved.reshape(moved.shape[:-2] + (F,))
    return (merge_wide(results[0]), merge_wide(results[1]), merge_wide(results[2]), merge_wide(results[3]))
```

```python
import math

import jax
import jax.numpy as jnp
import numpy as np
from jax import lax
from jax.experimental import pallas as pl
from jax.experimental.pallas import tpu as pltpu
from jax.sharding import PartitionSpec as P

F32 = jnp.float32
BF16 = jnp.bfloat16
VMEM = pl.BlockSpec(memory_space=pltpu.VMEM)
LIMIT = 48 * 1024 * 1024


def two_parts(table):
    high = table.astype(jnp.bfloat16)
    low = (table - high.astype(np.float64)).astype(jnp.bfloat16)
    return high, low


def make_tables(rows, blocks):
    kappa = np.arange(blocks)[:, None]
    block = np.arange(blocks)[None, :]
    angle = math.pi / (2 * blocks) * ((2 * kappa + 1) * block % (4 * blocks))
    stage1 = np.concatenate([np.cos(angle), -np.sin(angle)], axis=0)
    row = np.arange(rows)[None, :]
    turn = math.pi / (2 * rows * blocks) * ((2 * kappa + 1) * row % (4 * rows * blocks))
    k = np.arange(rows)[None, :]
    angle = 2 * math.pi / rows * (np.arange(rows)[:, None] * k % rows)
    cos, sin = np.cos(angle), np.sin(angle)
    stage2 = np.concatenate(
        [np.concatenate([cos, -sin], axis=1), np.concatenate([sin, cos], axis=1)], axis=0
    )
    back1 = stage1.T / (rows * blocks)
    back2 = stage2.T
    parts = []
    for table in (stage1, stage2, back1, back2):
        parts.extend(two_parts(table))
    return tuple(parts) + (np.cos(turn).astype(np.float32), np.sin(turn).astype(np.float32))


def split(x):
    high = x.astype(BF16)
    return high, (x - high.astype(F32)).astype(BF16)


def dot(a, b):
    return jnp.dot(a, b, preferred_element_type=F32)


def left_dot(high, low, x):
    x_high, x_low = split(x)
    return dot(high, x_high) + dot(high, x_low) + dot(low, x_high)


def right_dot(x, high, low):
    x_high, x_low = split(x)
    return dot(x_high, high) + dot(x_low, high) + dot(x_high, low)


def lanes(x, index, width=128):
    return x[:, index * width:(index + 1) * width]


def transform(x_ref, first, count, stride, exact, w_high, w_low, m_high, m_low, tc, ts):
    blocks = w_high.shape[1]
    columns = [x_ref[pl.ds(first + c, blocks, stride=stride), :] for c in range(count)]
    x = jnp.concatenate(columns, axis=1)
    if exact:
        x = x.astype(BF16)
        a = dot(w_high[...], x) + dot(w_low[...], x)
    else:
        a = left_dot(w_high[...], w_low[...], x)
    re, im = a[:blocks], a[blocks:]
    pieces = []
    for c in range(count):
        cr, ci = lanes(re, c), lanes(im, c)
        pieces.append(
            jnp.concatenate([cr * tc + ci * ts, ci * tc - cr * ts], axis=1)
        )
    return right_dot(jnp.concatenate(pieces, axis=0), m_high[...], m_low[...])


def inverse(spectra, w_high, w_low, m_high, m_low, tc, ts):
    blocks = w_high.shape[0]
    count = spectra.shape[0] // blocks
    c = right_dot(spectra, m_high[...], m_low[...])
    pieces = []
    for i in range(count):
        part = c[i * blocks:(i + 1) * blocks]
        cr, ci = lanes(part, 0), lanes(part, 1)
        pieces.append(
            jnp.concatenate([cr * tc - ci * ts, cr * ts + ci * tc], axis=0)
        )
    return left_dot(w_high[...], w_low[...], jnp.concatenate(pieces, axis=1))


def pack_kernel(group, parts, gate_ref, value_ref, cot_ref, filt_ref, out_ref):
    rows = gate_ref.shape[0]
    stride = out_ref.shape[0] // rows
    scale = 1.0 / math.sqrt(rows * rows)
    width = group * parts
    for c in range(parts):
        out_ref[pl.ds(width + c, rows, stride=stride), :] = (
            lanes(filt_ref, c).astype(F32) * scale
        ).T
    for c in range(width):
        out_ref[pl.ds(c, rows, stride=stride), :] = lanes(value_ref, c).astype(F32).T
    for c in range(width):
        gated = lanes(gate_ref, c).astype(F32) * lanes(cot_ref, c).astype(F32)
        out_ref[pl.ds(width + parts + c, rows, stride=stride), :] = gated.T


def spectra_kernel(
    group, parts, scale, x_ref, w1h, w1l, m2h, m2l, b1h, b1l, n2h, n2l, tcr, tsr,
    hs_ref, vs_ref, gs_ref, dh_ref,
):
    blocks = w1h.shape[1]
    stride = x_ref.shape[0] // blocks
    width = group * parts
    tc, ts = tcr[...], tsr[...]
    fwd = (w1h, w1l, m2h, m2l, tc, ts)
    vs_ref[...] = transform(x_ref, 0, width, stride, True, *fwd)
    gs_ref[...] = transform(x_ref, width + parts, width, stride, False, *fwd)
    pieces = []
    for q in range(parts):
        total_re = total_im = 0.0
        for s in range(group):
            at = pl.ds((s * parts + q) * blocks, blocks)
            v, g = vs_ref[at, :], gs_ref[at, :]
            vr, vi, gr, gi = lanes(v, 0), lanes(v, 1), lanes(g, 0), lanes(g, 1)
            total_re += gr * vr + gi * vi
            total_im += gi * vr - gr * vi
        pieces.append(jnp.concatenate([total_re, total_im], axis=1))
    dh = inverse(jnp.concatenate(pieces, axis=0), b1h, b1l, n2h, n2l, tc, ts)
    for q in range(parts):
        dh_ref[q] = lanes(dh, q) * scale
    hs_ref[...] = transform(x_ref, width, parts, stride, True, *fwd)


def products_kernel(
    group, parts, hs_ref, vs_ref, gs_ref, b1h, b1l, n2h, n2l, tcr, tsr, out_ref
):
    blocks = b1h.shape[0]
    stride = out_ref.shape[0] // blocks
    width = group * parts
    inv = (b1h, b1l, n2h, n2l, tcr[...], tsr[...])
    for which, ref in enumerate((vs_ref, gs_ref)):
        sign = 1.0 if which == 0 else -1.0
        pieces = []
        for c in range(width):
            x = ref[pl.ds(c * blocks, blocks), :]
            h = hs_ref[pl.ds((c % parts) * blocks, blocks), :]
            xr, xi, hr, hi = lanes(x, 0), lanes(x, 1), lanes(h, 0), lanes(h, 1) * sign
            pieces.append(jnp.concatenate([xr * hr - xi * hi, xr * hi + xi * hr], axis=1))
        y = inverse(jnp.concatenate(pieces, axis=0), *inv)
        for c in range(width):
            out_ref[pl.ds(which * width + c, blocks, stride=stride), :] = lanes(y, c)


def merge_kernel(dh_ref, big_ref, out_ref):
    parts, blocks, rows = dh_ref.shape
    stride = out_ref.shape[0] // blocks
    out_ref[...] = big_ref[...]
    total = dh_ref[0]
    for q in range(1, parts):
        total += dh_ref[q]
    out_ref[pl.ds(stride - 1, blocks, stride=stride), :] = total


def unpack_kernel(
    group, parts, x_ref, gate_ref, cot_ref, out_ref, gate_grad_ref, value_grad_ref, filt_ref
):
    rows = gate_ref.shape[0]
    stride = x_ref.shape[0] // rows
    width = group * parts
    for c in range(width):
        at = pl.ds(c * 128, 128)
        conv = x_ref[pl.ds(c, rows, stride=stride), :].T
        out_ref[:, at] = (gate_ref[:, at].astype(F32) * conv).astype(BF16)
        gate_grad_ref[:, at] = (cot_ref[:, at].astype(F32) * conv).astype(BF16)
        value_grad_ref[:, at] = x_ref[pl.ds(width + c, rows, stride=stride), :].T.astype(BF16)
    filt_ref[...] = x_ref[pl.ds(2 * width, rows, stride=stride), :].T.astype(BF16)


def call(body, outs, *args, **kw):
    return pl.pallas_call(
        body,
        out_shape=outs,
        in_specs=[VMEM] * len(args),
        out_specs=jax.tree.map(lambda _: VMEM, outs),
        compiler_params=pltpu.CompilerParams(vmem_limit_bytes=LIMIT),
        **kw,
    )(*args)


def exchange(x, blocks):
    flat = x.reshape(blocks, -1)
    return lax.all_to_all(flat, "seq", split_axis=0, concat_axis=0, tiled=True).reshape(x.shape)


def per_device(gate, value, filt, cotangent):
    rows, group, filters = value.shape
    blocks = lax.axis_size("seq")
    parts = filters // blocks
    width = group * parts
    w1h, w1l, m2h, m2l, b1h, b1l, n2h, n2l, tc, ts = make_tables(rows, blocks)
    gate = gate.reshape(rows, group * filters)
    value = value.reshape(rows, group * filters)
    cotangent = cotangent.reshape(rows, group * filters)

    def shape(*dims, dtype=F32):
        return jax.ShapeDtypeStruct(dims, dtype)

    sent = call(
        lambda *refs: pack_kernel(group, parts, *refs),
        shape(blocks * (2 * width + parts), rows),
        gate, value, cotangent, filt,
    )
    held = exchange(sent, blocks)
    scale = 1.0 / math.sqrt(rows * blocks)
    hs, vs, gs, dh = call(
        lambda *refs: spectra_kernel(group, parts, scale, *refs),
        (
            shape(parts * blocks, 2 * rows),
            shape(width * blocks, 2 * rows),
            shape(width * blocks, 2 * rows),
            shape(parts, blocks, rows),
        ),
        held, w1h, w1l, m2h, m2l, b1h, b1l, n2h, n2l, tc, ts,
    )
    dh = lax.all_to_all(dh, "ch", split_axis=0, concat_axis=0, tiled=True)
    big = call(
        lambda *refs: products_kernel(group, parts, *refs),
        shape(blocks * (2 * width + 1), rows),
        hs, vs, gs, b1h, b1l, n2h, n2l, tc, ts,
    )
    big = call(
        merge_kernel,
        shape(blocks * (2 * width + 1), rows),
        dh, big,
    )
    back = exchange(big, blocks)
    token = shape(rows, group * filters, dtype=BF16)
    out, gate_grad, value_grad, filt_grad = call(
        lambda *refs: unpack_kernel(group, parts, *refs),
        (token, token, token, shape(rows, blocks, dtype=BF16)),
        back, gate, cotangent,
    )
    full = (rows, group, filters)
    return out.reshape(full), gate_grad.reshape(full), value_grad.reshape(full), filt_grad


def solution(mesh):
    return jax.shard_map(
        per_device,
        mesh=mesh,
        in_specs=(P("seq", "ch", None), P("seq", "ch", None), P("seq", None), P("seq", "ch", None)),
        out_specs=(
            P("seq", "ch", None),
            P("seq", "ch", None),
            P("seq", "ch", None),
            P("seq", "ch"),
        ),
        check_vma=False,
    )
```

```python
import math

import jax
import jax.numpy as jnp
import numpy as np
from jax import lax
from jax.experimental import pallas as pl
from jax.experimental.pallas import tpu as pltpu
from jax.sharding import PartitionSpec as P

F32 = jnp.float32
BF16 = jnp.bfloat16
VMEM = pl.BlockSpec(memory_space=pltpu.VMEM)
LIMIT = 24 * 1024 * 1024


def two_parts(table):
    high = table.astype(jnp.bfloat16)
    low = (table - high.astype(np.float64)).astype(jnp.bfloat16)
    return high, low


def make_tables(rows, blocks):
    kappa = np.arange(blocks)[:, None]
    block = np.arange(blocks)[None, :]
    angle = math.pi / (2 * blocks) * ((2 * kappa + 1) * block % (4 * blocks))
    stage1 = np.concatenate([np.cos(angle), -np.sin(angle)], axis=0)
    row = np.arange(rows)[None, :]
    turn = math.pi / (2 * rows * blocks) * ((2 * kappa + 1) * row % (4 * rows * blocks))
    k = np.arange(rows)[None, :]
    angle = 2 * math.pi / rows * (np.arange(rows)[:, None] * k % rows)
    cos, sin = np.cos(angle), np.sin(angle)
    stage2 = np.concatenate(
        [np.concatenate([cos, -sin], axis=1), np.concatenate([sin, cos], axis=1)], axis=0
    )
    back1 = stage1.T / (rows * blocks)
    back2 = stage2.T
    parts = []
    for table in (stage1, stage2, back1, back2):
        parts.extend(two_parts(table))
    return tuple(parts) + (np.cos(turn).astype(np.float32), np.sin(turn).astype(np.float32))


def split(x):
    high = x.astype(BF16)
    return high, (x - high.astype(F32)).astype(BF16)


def dot(a, b):
    return jnp.dot(a, b, preferred_element_type=F32)


def left_dot(high, low, x):
    x_high, x_low = split(x)
    return dot(high, x_high) + dot(high, x_low) + dot(low, x_high)


def right_dot(x, high, low):
    x_high, x_low = split(x)
    return dot(x_high, high) + dot(x_low, high) + dot(x_high, low)


def lanes(x, index, width=128):
    return x[:, index * width:(index + 1) * width]


def transform(x_ref, first, count, stride, exact, pair, high, m_high, m_low, tc, ts):
    blocks = high.shape[1]
    columns = [x_ref[pl.ds(first + c, blocks, stride=stride), :] for c in range(count)]
    x = jnp.concatenate(columns, axis=1)
    if exact:
        x = x.astype(BF16)
        a = dot(pair[...], jnp.concatenate([x, x], axis=0))
    else:
        x, low = split(x)
        a = dot(pair[...], jnp.concatenate([x, x], axis=0)) + dot(high[...], low)
    re, im = a[:blocks], a[blocks:]
    pieces = []
    for c in range(count):
        cr, ci = lanes(re, c), lanes(im, c)
        pieces.append(
            jnp.concatenate([cr * tc + ci * ts, ci * tc - cr * ts], axis=1)
        )
    return right_dot(jnp.concatenate(pieces, axis=0), m_high[...], m_low[...])


def inverse(spectra, w_high, w_low, m_high, m_low, tc, ts):
    blocks = w_high.shape[0]
    count = spectra.shape[0] // blocks
    c = right_dot(spectra, m_high[...], m_low[...])
    pieces = []
    for i in range(count):
        part = c[i * blocks:(i + 1) * blocks]
        cr, ci = lanes(part, 0), lanes(part, 1)
        pieces.append(
            jnp.concatenate([cr * tc - ci * ts, cr * ts + ci * tc], axis=0)
        )
    return left_dot(w_high[...], w_low[...], jnp.concatenate(pieces, axis=1))


def pack_kernel(width, parts, gate_ref, value_ref, cot_ref, filt_ref, out_ref, v_ref, g_ref):
    rows = filt_ref.shape[0]
    stride = out_ref.shape[0] // rows
    scale = 1.0 / math.sqrt(rows * rows)
    v_ref[...] = value_ref[...].astype(F32)
    g_ref[...] = cot_ref[...].astype(F32) * gate_ref[...].astype(F32)
    for c in range(width):
        at = pl.ds(c, rows, stride=width)
        out_ref[pl.ds(c, rows, stride=stride), :] = v_ref[at, :].T
        out_ref[pl.ds(width + c, rows, stride=stride), :] = g_ref[at, :].T
    for c in range(parts):
        out_ref[pl.ds(2 * width + c, rows, stride=stride), :] = (
            lanes(filt_ref, c).astype(F32) * scale
        ).T


def spectra_kernel(
    group, parts, scale, x_ref, pair, w1h, m2h, m2l, b1h, b1l, n2h, n2l, tcr, tsr,
    dh_ref, vs_ref, gs_ref,
):
    blocks = w1h.shape[1]
    stride = x_ref.shape[0] // blocks
    width = group * parts
    tc, ts = tcr[...], tsr[...]
    fwd = (pair, w1h, m2h, m2l, tc, ts)
    vs_ref[...] = transform(x_ref, 0, width, stride, True, *fwd)
    gs_ref[...] = transform(x_ref, width, width, stride, False, *fwd)
    pieces = []
    for q in range(parts):
        total_re = total_im = 0.0
        for s in range(group):
            at = pl.ds((q * group + s) * blocks, blocks)
            v, g = vs_ref[at, :], gs_ref[at, :]
            vr, vi, gr, gi = lanes(v, 0), lanes(v, 1), lanes(g, 0), lanes(g, 1)
            total_re += gr * vr + gi * vi
            total_im += gi * vr - gr * vi
        pieces.append(jnp.concatenate([total_re, total_im], axis=1))
    dh = inverse(jnp.concatenate(pieces, axis=0), b1h, b1l, n2h, n2l, tc, ts)
    for q in range(parts):
        dh_ref[q] = lanes(dh, q) * scale


def products_kernel(
    group, parts, x_ref, pair, w1h, m2h, m2l, b1h, b1l, n2h, n2l, tcr, tsr, out_ref
):
    blocks = w1h.shape[1]
    stride = out_ref.shape[0] // blocks
    width = group * parts
    tc, ts = tcr[...], tsr[...]
    held = x_ref.shape[0] // blocks
    fwd = (pair, w1h, m2h, m2l, tc, ts)
    inv = (b1h, b1l, n2h, n2l, tc, ts)
    spectra = transform(x_ref, 2 * width, parts, held, True, *fwd)
    for which in range(2):
        signal = transform(x_ref, which * width, width, held, which == 0, *fwd)
        sign = 1.0 if which == 0 else -1.0
        pieces = []
        for c in range(width):
            x = signal[c * blocks:(c + 1) * blocks]
            q = c // group
            h = spectra[q * blocks:(q + 1) * blocks]
            xr, xi, hr, hi = lanes(x, 0), lanes(x, 1), lanes(h, 0), lanes(h, 1) * sign
            pieces.append(jnp.concatenate([xr * hr - xi * hi, xr * hi + xi * hr], axis=1))
        y = inverse(jnp.concatenate(pieces, axis=0), *inv)
        for c in range(width):
            out_ref[pl.ds(which * width + c, blocks, stride=stride), :] = lanes(y, c)


def merge_kernel(dh_ref, big_ref, out_ref):
    parts, blocks, rows = dh_ref.shape
    stride = out_ref.shape[0] // blocks
    out_ref[...] = big_ref[...]
    total = dh_ref[0]
    for q in range(1, parts):
        total += dh_ref[q]
    out_ref[pl.ds(stride - 1, blocks, stride=stride), :] = total


def unpack_kernel(
    width, x_ref, gate_ref, cot_ref, out_ref, gate_grad_ref, value_grad_ref, filt_ref,
    conv_ref, grad_ref,
):
    rows = filt_ref.shape[0]
    stride = x_ref.shape[0] // rows
    for c in range(width):
        at = pl.ds(c, rows, stride=width)
        conv_ref[at, :] = x_ref[pl.ds(c, rows, stride=stride), :].T
        grad_ref[at, :] = x_ref[pl.ds(width + c, rows, stride=stride), :].T
    conv = conv_ref[...]
    out_ref[...] = (gate_ref[...].astype(F32) * conv).astype(BF16)
    gate_grad_ref[...] = (cot_ref[...].astype(F32) * conv).astype(BF16)
    value_grad_ref[...] = grad_ref[...].astype(BF16)
    filt_ref[...] = x_ref[pl.ds(2 * width, rows, stride=stride), :].T.astype(BF16)


def call(body, outs, *args, **kw):
    return pl.pallas_call(
        body,
        out_shape=outs,
        in_specs=[VMEM] * len(args),
        out_specs=jax.tree.map(lambda _: VMEM, outs),
        compiler_params=pltpu.CompilerParams(vmem_limit_bytes=LIMIT),
        **kw,
    )(*args)


def exchange(x, blocks):
    flat = x.reshape(blocks, -1)
    return lax.all_to_all(flat, "seq", split_axis=0, concat_axis=0, tiled=True).reshape(x.shape)


def per_device(gate, value, filt, cotangent):
    rows, group, filters = value.shape
    blocks = lax.axis_size("seq")
    parts = filters // blocks
    width = group * parts
    w1h, w1l, m2h, m2l, b1h, b1l, n2h, n2l, tc, ts = make_tables(rows, blocks)
    pair = np.concatenate([w1h, w1l], axis=1)
    forward, backward, turns = (pair, w1h, m2h, m2l), (b1h, b1l, n2h, n2l), (tc, ts)

    def to_rows(x):
        x = x.reshape(rows, group, parts, blocks).transpose(0, 2, 1, 3)
        return x.reshape(rows * width, blocks)

    def from_rows(x):
        x = x.reshape(rows, parts, group, blocks).transpose(0, 2, 1, 3)
        return x.reshape(rows, group, filters)

    def shape(*dims, dtype=F32):
        return jax.ShapeDtypeStruct(dims, dtype)

    gate, value, cotangent = to_rows(gate), to_rows(value), to_rows(cotangent)
    wide = pltpu.VMEM((rows * width, blocks), F32)
    sent = call(
        lambda *refs: pack_kernel(width, parts, *refs),
        shape(blocks * (2 * width + parts), rows),
        gate, value, cotangent, filt,
        scratch_shapes=[wide, wide],
    )
    held = exchange(sent, blocks)
    scale = 1.0 / math.sqrt(rows * blocks)
    spectra = pltpu.VMEM((width * blocks, 2 * rows), F32)
    dh = call(
        lambda *refs: spectra_kernel(group, parts, scale, *refs),
        shape(parts, blocks, rows),
        held, *forward, *backward, *turns,
        scratch_shapes=[spectra, spectra],
    )
    dh = lax.all_to_all(dh, "ch", split_axis=0, concat_axis=0, tiled=True)
    big = call(
        lambda *refs: products_kernel(group, parts, *refs),
        shape(blocks * (2 * width + 1), rows),
        held, *forward, *backward, *turns,
    )
    big = call(
        merge_kernel,
        shape(blocks * (2 * width + 1), rows),
        dh, big,
    )
    back = exchange(big, blocks)
    token = shape(rows * width, blocks, dtype=BF16)
    out, gate_grad, value_grad, filt_grad = call(
        lambda *refs: unpack_kernel(width, *refs),
        (token, token, token, shape(rows, blocks, dtype=BF16)),
        back, gate, cotangent,
        scratch_shapes=[wide, wide],
    )
    return from_rows(out), from_rows(gate_grad), from_rows(value_grad), filt_grad


def solution(mesh):
    return jax.shard_map(
        per_device,
        mesh=mesh,
        in_specs=(P("seq", "ch", None), P("seq", "ch", None), P("seq", None), P("seq", "ch", None)),
        out_specs=(
            P("seq", "ch", None),
            P("seq", "ch", None),
            P("seq", "ch", None),
            P("seq", "ch"),
        ),
        check_vma=False,
    )
```

```python
import math

import jax
import jax.numpy as jnp
import numpy as np
from jax import lax
from jax.experimental import pallas as pl
from jax.experimental.pallas import tpu as pltpu
from jax.sharding import PartitionSpec as P

F32 = jnp.float32
BF16 = jnp.bfloat16
VMEM = pl.BlockSpec(memory_space=pltpu.VMEM)
HBM = pl.BlockSpec(memory_space=pltpu.HBM)
MIB = 1024 * 1024


def two_parts(table):
    high = table.astype(jnp.bfloat16)
    low = (table - high.astype(np.float64)).astype(jnp.bfloat16)
    return high, low


def make_tables(rows, blocks):
    kappa = np.arange(blocks)[:, None]
    block = np.arange(blocks)[None, :]
    angle = math.pi / (2 * blocks) * ((2 * kappa + 1) * block % (4 * blocks))
    stage1 = np.concatenate([np.cos(angle), -np.sin(angle)], axis=0)
    row = np.arange(rows)[None, :]
    turn = math.pi / (2 * rows * blocks) * ((2 * kappa + 1) * row % (4 * rows * blocks))
    k = np.arange(rows)[None, :]
    angle = 2 * math.pi / rows * (np.arange(rows)[:, None] * k % rows)
    cos, sin = np.cos(angle), np.sin(angle)
    stage2 = np.concatenate(
        [np.concatenate([cos, -sin], axis=1), np.concatenate([sin, cos], axis=1)], axis=0
    )
    back1 = stage1.T / (rows * blocks)
    back2 = stage2.T
    pieces = [np.concatenate(two_parts(stage1), axis=1)]
    for table in (stage2, back2, back1):
        pieces.extend(two_parts(table))
    pieces.extend(two_parts(np.concatenate([np.cos(turn), np.sin(turn)], axis=1)))
    return np.concatenate(pieces, axis=0)


class Tables:
    def __init__(self, table_ref):
        full = table_ref.shape[1]
        blocks = full // 2

        def rows(first, count, lanes=full):
            return table_ref[pl.ds(first, count), pl.ds(0, lanes)]

        self.blocks = blocks
        self.pair = lambda: rows(0, full)
        self.stage1_high = lambda: rows(0, full, blocks)
        self.stage2 = lambda: (rows(full, full), rows(2 * full, full))
        self.back2 = lambda: (rows(3 * full, full), rows(4 * full, full))
        self.back1 = lambda: (rows(5 * full, blocks), rows(5 * full + blocks, blocks))
        turn = rows(6 * full, blocks).astype(F32) + rows(6 * full + blocks, blocks).astype(F32)
        self.cos, self.sin = turn[:, :blocks], turn[:, blocks:]


def split(x):
    high = x.astype(BF16)
    return high, (x - high.astype(F32)).astype(BF16)


def dot(a, b):
    return jnp.dot(a, b, preferred_element_type=F32)


def left_dot(high, low, x):
    x_high, x_low = split(x)
    return dot(high, x_high) + dot(high, x_low) + dot(low, x_high)


def right_dot(x, high, low):
    x_high, x_low = split(x)
    return dot(x_high, high) + dot(x_low, high) + dot(x_high, low)


def lanes(x, index, width=128):
    return x[:, index * width:(index + 1) * width]


def transform(x_ref, first, count, stride, exact, tables):
    blocks, tc, ts = tables.blocks, tables.cos, tables.sin
    columns = [x_ref[pl.ds(first + c, blocks, stride=stride), :] for c in range(count)]
    x = jnp.concatenate(columns, axis=1)
    if exact:
        x = x.astype(BF16)
        a = dot(tables.pair(), jnp.concatenate([x, x], axis=0))
    else:
        x, low = split(x)
        a = dot(tables.pair(), jnp.concatenate([x, x], axis=0)) + dot(tables.stage1_high(), low)
    re, im = a[:blocks], a[blocks:]
    pieces = []
    for c in range(count):
        cr, ci = lanes(re, c), lanes(im, c)
        pieces.append(
            jnp.concatenate([cr * tc + ci * ts, ci * tc - cr * ts], axis=1)
        )
    return right_dot(jnp.concatenate(pieces, axis=0), *tables.stage2())


def inverse(spectra, tables):
    blocks, tc, ts = tables.blocks, tables.cos, tables.sin
    count = spectra.shape[0] // blocks
    c = right_dot(spectra, *tables.back2())
    pieces = []
    for i in range(count):
        part = c[i * blocks:(i + 1) * blocks]
        cr, ci = lanes(part, 0), lanes(part, 1)
        pieces.append(
            jnp.concatenate([cr * tc - ci * ts, cr * ts + ci * tc], axis=0)
        )
    return left_dot(*tables.back1(), jnp.concatenate(pieces, axis=1))


def pack_kernel(
    width, parts, gate_hbm, value_hbm, cot_hbm, filt_hbm, out_ref,
    gate_ref, value_ref, cot_ref, filt_ref, v_ref, g_ref, sems,
):
    pairs = ((value_hbm, value_ref), (gate_hbm, gate_ref), (cot_hbm, cot_ref), (filt_hbm, filt_ref))
    copies = [pltpu.make_async_copy(a, b, sems.at[i]) for i, (a, b) in enumerate(pairs)]
    for copy in copies:
        copy.start()
    rows = filt_ref.shape[0]
    stride = out_ref.shape[0] // rows
    scale = 1.0 / math.sqrt(rows * rows)
    copies[0].wait()
    v_ref[...] = value_ref[...].astype(F32)
    for c in range(width):
        out_ref[pl.ds(c, rows, stride=stride), :] = v_ref[pl.ds(c, rows, stride=width), :].T
    copies[1].wait()
    copies[2].wait()
    g_ref[...] = cot_ref[...].astype(F32) * gate_ref[...].astype(F32)
    for c in range(width):
        out_ref[pl.ds(width + c, rows, stride=stride), :] = g_ref[pl.ds(c, rows, stride=width), :].T
    copies[3].wait()
    for c in range(parts):
        out_ref[pl.ds(2 * width + c, rows, stride=stride), :] = (
            lanes(filt_ref, c).astype(F32) * scale
        ).T


def spectra_kernel(
    group, parts, scale, x_ref, table_ref, dh_ref, vs_ref, gs_ref
):
    tables = Tables(table_ref)
    blocks = tables.blocks
    stride = x_ref.shape[0] // blocks
    width = group * parts
    vs_ref[...] = transform(x_ref, 0, width, stride, True, tables)
    gs_ref[...] = transform(x_ref, width, width, stride, False, tables)
    pieces = []
    for q in range(parts):
        total_re = total_im = 0.0
        for s in range(group):
            at = pl.ds((q * group + s) * blocks, blocks)
            v, g = vs_ref[at, :], gs_ref[at, :]
            vr, vi, gr, gi = lanes(v, 0), lanes(v, 1), lanes(g, 0), lanes(g, 1)
            total_re += gr * vr + gi * vi
            total_im += gi * vr - gr * vi
        pieces.append(jnp.concatenate([total_re, total_im], axis=1))
    dh = inverse(jnp.concatenate(pieces, axis=0), tables)
    for q in range(parts):
        dh_ref[q] = lanes(dh, q) * scale


def products_kernel(group, parts, x_ref, table_ref, out_ref):
    tables = Tables(table_ref)
    blocks = tables.blocks
    stride = out_ref.shape[0] // blocks
    width = group * parts
    held = x_ref.shape[0] // blocks
    spectra = transform(x_ref, 2 * width, parts, held, True, tables)
    for which in range(2):
        signal = transform(x_ref, which * width, width, held, which == 0, tables)
        sign = 1.0 if which == 0 else -1.0
        pieces = []
        for c in range(width):
            x = signal[c * blocks:(c + 1) * blocks]
            q = c // group
            h = spectra[q * blocks:(q + 1) * blocks]
            xr, xi, hr, hi = lanes(x, 0), lanes(x, 1), lanes(h, 0), lanes(h, 1) * sign
            pieces.append(jnp.concatenate([xr * hr - xi * hi, xr * hi + xi * hr], axis=1))
        y = inverse(jnp.concatenate(pieces, axis=0), tables)
        for c in range(width):
            out_ref[pl.ds(which * width + c, blocks, stride=stride), :] = lanes(y, c)


def merge_kernel(dh_ref, big_ref, out_ref):
    parts, blocks, rows = dh_ref.shape
    stride = out_ref.shape[0] // blocks
    out_ref[...] = big_ref[...]
    total = dh_ref[0]
    for q in range(1, parts):
        total += dh_ref[q]
    out_ref[pl.ds(stride - 1, blocks, stride=stride), :] = total


def unpack_kernel(
    width, x_ref, gate_ref, cot_ref, out_ref, gate_grad_ref, value_grad_ref, filt_ref,
    conv_ref, grad_ref,
):
    rows = filt_ref.shape[0]
    stride = x_ref.shape[0] // rows
    for c in range(width):
        at = pl.ds(c, rows, stride=width)
        conv_ref[at, :] = x_ref[pl.ds(c, rows, stride=stride), :].T
        grad_ref[at, :] = x_ref[pl.ds(width + c, rows, stride=stride), :].T
    conv = conv_ref[...]
    out_ref[...] = (gate_ref[...].astype(F32) * conv).astype(BF16)
    gate_grad_ref[...] = (cot_ref[...].astype(F32) * conv).astype(BF16)
    value_grad_ref[...] = grad_ref[...].astype(BF16)
    filt_ref[...] = x_ref[pl.ds(2 * width, rows, stride=stride), :].T.astype(BF16)


def call(body, outs, *args, space=VMEM, limit=24 * MIB, **kw):
    return pl.pallas_call(
        body,
        out_shape=outs,
        in_specs=[space] * len(args),
        out_specs=jax.tree.map(lambda _: VMEM, outs),
        compiler_params=pltpu.CompilerParams(vmem_limit_bytes=limit),
        **kw,
    )(*args)


def exchange(x, blocks):
    flat = x.reshape(blocks, -1)
    return lax.all_to_all(flat, "seq", split_axis=0, concat_axis=0, tiled=True).reshape(x.shape)


def per_device(gate, value, filt, cotangent):
    rows, group, filters = value.shape
    blocks = lax.axis_size("seq")
    parts = filters // blocks
    width = group * parts
    tables = make_tables(rows, blocks)

    def to_rows(x):
        x = x.reshape(rows, group, parts, blocks).transpose(0, 2, 1, 3)
        return x.reshape(rows * width, blocks)

    def from_rows(x):
        x = x.reshape(rows, parts, group, blocks).transpose(0, 2, 1, 3)
        return x.reshape(rows, group, filters)

    def shape(*dims, dtype=F32):
        return jax.ShapeDtypeStruct(dims, dtype)

    gate, value, cotangent = to_rows(gate), to_rows(value), to_rows(cotangent)
    wide = pltpu.VMEM((rows * width, blocks), F32)
    sent = call(
        lambda *refs: pack_kernel(width, parts, *refs),
        shape(blocks * (2 * width + parts), rows),
        gate, value, cotangent, filt,
        space=HBM,
        limit=62 * MIB,
        scratch_shapes=[
            *[pltpu.VMEM((rows * width, blocks), BF16)] * 3,
            pltpu.VMEM((rows, filters), BF16),
            wide,
            wide,
            pltpu.SemaphoreType.DMA((4,)),
        ],
    )
    held = exchange(sent, blocks)
    scale = 1.0 / math.sqrt(rows * blocks)
    spectra = pltpu.VMEM((width * blocks, 2 * rows), F32)
    dh = call(
        lambda *refs: spectra_kernel(group, parts, scale, *refs),
        shape(parts, blocks, rows),
        held, tables,
        scratch_shapes=[spectra, spectra],
    )
    dh = lax.all_to_all(dh, "ch", split_axis=0, concat_axis=0, tiled=True)
    big = call(
        lambda *refs: products_kernel(group, parts, *refs),
        shape(blocks * (2 * width + 1), rows),
        held, tables,
    )
    big = call(
        merge_kernel,
        shape(blocks * (2 * width + 1), rows),
        dh, big,
        limit=6 * MIB,
    )
    back = exchange(big, blocks)
    token = shape(rows * width, blocks, dtype=BF16)
    out, gate_grad, value_grad, filt_grad = call(
        lambda *refs: unpack_kernel(width, *refs),
        (token, token, token, shape(rows, blocks, dtype=BF16)),
        back, gate, cotangent,
        limit=10 * MIB,
        scratch_shapes=[wide, wide],
    )
    return from_rows(out), from_rows(gate_grad), from_rows(value_grad), filt_grad


def solution(mesh):
    return jax.shard_map(
        per_device,
        mesh=mesh,
        in_specs=(P("seq", "ch", None), P("seq", "ch", None), P("seq", None), P("seq", "ch", None)),
        out_specs=(
            P("seq", "ch", None),
            P("seq", "ch", None),
            P("seq", "ch", None),
            P("seq", "ch"),
        ),
        check_vma=False,
    )
```

```python
import math

import jax
import jax.numpy as jnp
import numpy as np
from jax import lax
from jax.experimental import pallas as pl
from jax.experimental.pallas import tpu as pltpu
from jax.sharding import PartitionSpec as P

F32 = jnp.float32
BF16 = jnp.bfloat16
VMEM = pl.BlockSpec(memory_space=pltpu.VMEM)
HBM = pl.BlockSpec(memory_space=pltpu.HBM)
MIB = 1024 * 1024
STRIDE = 19


def two_parts(table):
    high = table.astype(jnp.bfloat16)
    low = (table - high.astype(np.float64)).astype(jnp.bfloat16)
    return high, low


def make_tables(rows, blocks, order):
    kappa = np.arange(blocks)[:, None]
    block = np.arange(blocks)[None, :]
    angle = math.pi / (2 * blocks) * ((2 * kappa + 1) * block % (4 * blocks))
    stage1 = np.concatenate([np.cos(angle), -np.sin(angle)], axis=0)
    row = np.arange(rows)[None, :]
    turn = math.pi / (2 * rows * blocks) * ((2 * kappa + 1) * row % (4 * rows * blocks))
    k = np.arange(rows)[None, :]
    angle = 2 * math.pi / rows * (np.arange(rows)[:, None] * k % rows)
    cos, sin = np.cos(angle), np.sin(angle)
    stage2 = np.concatenate(
        [np.concatenate([cos, -sin], axis=1), np.concatenate([sin, cos], axis=1)], axis=0
    )
    stage1 = stage1[:, order]
    back1 = stage1.T / (rows * blocks)
    back2 = stage2.T
    pieces = [np.concatenate(two_parts(stage1), axis=1)]
    for table in (stage2, back2, back1):
        pieces.extend(two_parts(table))
    pieces.extend(two_parts(np.concatenate([np.cos(turn), np.sin(turn)], axis=1)))
    return np.concatenate(pieces, axis=0)


class Tables:
    def __init__(self, table_ref):
        full = table_ref.shape[1]
        blocks = full // 2

        def rows(first, count, lanes=full):
            return table_ref[pl.ds(first, count), pl.ds(0, lanes)]

        self.blocks = blocks
        self.pair = lambda: rows(0, full)
        self.stage1_high = lambda: rows(0, full, blocks)
        self.stage2 = lambda: (rows(full, full), rows(2 * full, full))
        self.back2 = lambda: (rows(3 * full, full), rows(4 * full, full))
        self.back1 = lambda: (rows(5 * full, blocks), rows(5 * full + blocks, blocks))
        turn = rows(6 * full, blocks).astype(F32) + rows(6 * full + blocks, blocks).astype(F32)
        self.cos, self.sin = turn[:, :blocks], turn[:, blocks:]


def split(x):
    high = x.astype(BF16)
    return high, (x - high.astype(F32)).astype(BF16)


def dot(a, b):
    return jnp.dot(a, b, preferred_element_type=F32)


def left_dot(high, low, x):
    x_high, x_low = split(x)
    return dot(high, x_high) + dot(high, x_low) + dot(low, x_high)


def right_dot(x, high, low):
    x_high, x_low = split(x)
    return dot(x_high, high) + dot(x_low, high) + dot(x_high, low)


def lanes(x, index, width=128):
    return x[:, index * width:(index + 1) * width]


def transform(x_ref, first, count, stride, exact, tables):
    blocks, tc, ts = tables.blocks, tables.cos, tables.sin
    columns = [x_ref[pl.ds(first + c, blocks, stride=stride), :] for c in range(count)]
    x = jnp.concatenate(columns, axis=1)
    if exact:
        x = x.astype(BF16)
        a = dot(tables.pair(), jnp.concatenate([x, x], axis=0))
    else:
        x, low = split(x)
        a = dot(tables.pair(), jnp.concatenate([x, x], axis=0)) + dot(tables.stage1_high(), low)
    re, im = a[:blocks], a[blocks:]
    pieces = []
    for c in range(count):
        cr, ci = lanes(re, c), lanes(im, c)
        pieces.append(
            jnp.concatenate([cr * tc + ci * ts, ci * tc - cr * ts], axis=1)
        )
    return right_dot(jnp.concatenate(pieces, axis=0), *tables.stage2())


def inverse(spectra, tables):
    blocks, tc, ts = tables.blocks, tables.cos, tables.sin
    count = spectra.shape[0] // blocks
    c = right_dot(spectra, *tables.back2())
    pieces = []
    for i in range(count):
        part = c[i * blocks:(i + 1) * blocks]
        cr, ci = lanes(part, 0), lanes(part, 1)
        pieces.append(
            jnp.concatenate([cr * tc - ci * ts, cr * ts + ci * tc], axis=0)
        )
    return left_dot(*tables.back1(), jnp.concatenate(pieces, axis=1))


def pack_kernel(
    width, parts, gate_hbm, value_hbm, cot_hbm, filt_hbm, out_ref,
    gate_ref, value_ref, cot_ref, filt_ref, v_ref, g_ref, sems,
):
    pairs = ((value_hbm, value_ref), (gate_hbm, gate_ref), (cot_hbm, cot_ref), (filt_hbm, filt_ref))
    copies = [pltpu.make_async_copy(a, b, sems.at[i]) for i, (a, b) in enumerate(pairs)]
    for copy in copies:
        copy.start()
    rows = filt_ref.shape[0]
    stride = out_ref.shape[0] // rows
    scale = 1.0 / math.sqrt(rows * rows)
    copies[0].wait()
    v_ref[...] = value_ref[...].astype(F32)
    for c in range(width):
        out_ref[pl.ds(c, rows, stride=stride), :] = v_ref[pl.ds(c, rows, stride=width), :].T
    copies[1].wait()
    copies[2].wait()
    g_ref[...] = cot_ref[...].astype(F32) * gate_ref[...].astype(F32)
    for c in range(width):
        out_ref[pl.ds(width + c, rows, stride=stride), :] = g_ref[pl.ds(c, rows, stride=width), :].T
    copies[3].wait()
    for c in range(parts):
        out_ref[pl.ds(2 * width + c, rows, stride=stride), :] = (
            lanes(filt_ref, c).astype(F32) * scale
        ).T


def spectra_kernel(
    group, parts, scale, x_ref, table_ref, dh_ref, vs_ref, gs_ref
):
    tables = Tables(table_ref)
    blocks = tables.blocks
    stride = x_ref.shape[0] // blocks
    width = group * parts
    vs_ref[...] = transform(x_ref, 0, width, stride, True, tables)
    gs_ref[...] = transform(x_ref, width, width, stride, False, tables)
    pieces = []
    for q in range(parts):
        total_re = total_im = 0.0
        for s in range(group):
            at = pl.ds((q * group + s) * blocks, blocks)
            v, g = vs_ref[at, :], gs_ref[at, :]
            vr, vi, gr, gi = lanes(v, 0), lanes(v, 1), lanes(g, 0), lanes(g, 1)
            total_re += gr * vr + gi * vi
            total_im += gi * vr - gr * vi
        pieces.append(jnp.concatenate([total_re, total_im], axis=1))
    dh = inverse(jnp.concatenate(pieces, axis=0), tables)
    for q in range(parts):
        dh_ref[q] = lanes(dh, q) * scale


def products_kernel(group, parts, x_ref, table_ref, out_ref):
    tables = Tables(table_ref)
    blocks = tables.blocks
    stride = out_ref.shape[0] // blocks
    width = group * parts
    held = x_ref.shape[0] // blocks
    spectra = transform(x_ref, 2 * width, parts, held, True, tables)
    for which in range(2):
        signal = transform(x_ref, which * width, width, held, which == 0, tables)
        sign = 1.0 if which == 0 else -1.0
        pieces = []
        for c in range(width):
            x = signal[c * blocks:(c + 1) * blocks]
            q = c // group
            h = spectra[q * blocks:(q + 1) * blocks]
            xr, xi, hr, hi = lanes(x, 0), lanes(x, 1), lanes(h, 0), lanes(h, 1) * sign
            pieces.append(jnp.concatenate([xr * hr - xi * hi, xr * hi + xi * hr], axis=1))
        y = inverse(jnp.concatenate(pieces, axis=0), tables)
        for c in range(width):
            out_ref[pl.ds(which * width + c, blocks, stride=stride), :] = lanes(y, c)


def merge_kernel(dh_ref, big_ref, out_ref):
    parts, blocks, rows = dh_ref.shape
    stride = out_ref.shape[0] // blocks
    out_ref[...] = big_ref[...]
    total = dh_ref[0]
    for q in range(1, parts):
        total += dh_ref[q]
    out_ref[pl.ds(stride - 1, blocks, stride=stride), :] = total


def unpack_kernel(
    width, x_ref, gate_ref, cot_ref, out_ref, gate_grad_ref, value_grad_ref, filt_ref,
    conv_ref, grad_ref,
):
    rows = filt_ref.shape[0]
    stride = x_ref.shape[0] // rows
    for c in range(width):
        at = pl.ds(c, rows, stride=width)
        conv_ref[at, :] = x_ref[pl.ds(c, rows, stride=stride), :].T
        grad_ref[at, :] = x_ref[pl.ds(width + c, rows, stride=stride), :].T
    conv = conv_ref[...]
    out_ref[...] = (gate_ref[...].astype(F32) * conv).astype(BF16)
    gate_grad_ref[...] = (cot_ref[...].astype(F32) * conv).astype(BF16)
    value_grad_ref[...] = grad_ref[...].astype(BF16)
    filt_ref[...] = x_ref[pl.ds(2 * width, rows, stride=stride), :].T.astype(BF16)


def call(body, outs, *args, space=VMEM, limit=24 * MIB, **kw):
    return pl.pallas_call(
        body,
        out_shape=outs,
        in_specs=[space] * len(args),
        out_specs=jax.tree.map(lambda _: VMEM, outs),
        compiler_params=pltpu.CompilerParams(vmem_limit_bytes=limit),
        **kw,
    )(*args)


def exchange(x, order):
    flat = x.reshape(len(order), -1)
    out = lax.all_to_all(
        flat, "seq", split_axis=0, concat_axis=0, axis_index_groups=[order], tiled=True
    )
    return out.reshape(x.shape)


def per_device(gate, value, filt, cotangent):
    rows, group, filters = value.shape
    blocks = lax.axis_size("seq")
    parts = filters // blocks
    width = group * parts
    order = [STRIDE * i % blocks for i in range(blocks)]
    tables = make_tables(rows, blocks, order)

    def to_rows(x):
        x = x.reshape(rows, group, parts, blocks).transpose(0, 2, 1, 3)
        return x.reshape(rows * width, blocks)

    def from_rows(x):
        x = x.reshape(rows, parts, group, blocks).transpose(0, 2, 1, 3)
        return x.reshape(rows, group, filters)

    def shape(*dims, dtype=F32):
        return jax.ShapeDtypeStruct(dims, dtype)

    gate, value, cotangent = to_rows(gate), to_rows(value), to_rows(cotangent)
    wide = pltpu.VMEM((rows * width, blocks), F32)
    sent = call(
        lambda *refs: pack_kernel(width, parts, *refs),
        shape(blocks * (2 * width + parts), rows),
        *[pltpu.with_memory_space_constraint(x, pltpu.HBM) for x in (gate, value, cotangent, filt)],
        space=HBM,
        limit=24 * MIB,
        scratch_shapes=[
            *[pltpu.VMEM((rows * width, blocks), BF16)] * 3,
            pltpu.VMEM((rows, filters), BF16),
            wide,
            wide,
            pltpu.SemaphoreType.DMA((4,)),
        ],
    )
    held = exchange(sent, order)
    scale = 1.0 / math.sqrt(rows * blocks)
    spectra = pltpu.VMEM((width * blocks, 2 * rows), F32)
    dh = call(
        lambda *refs: spectra_kernel(group, parts, scale, *refs),
        shape(parts, blocks, rows),
        held, tables,
        scratch_shapes=[spectra, spectra],
    )
    dh = lax.all_to_all(dh, "ch", split_axis=0, concat_axis=0, tiled=True)
    big = call(
        lambda *refs: products_kernel(group, parts, *refs),
        shape(blocks * (2 * width + 1), rows),
        held, tables,
    )
    big = call(
        merge_kernel,
        shape(blocks * (2 * width + 1), rows),
        dh, big,
        limit=6 * MIB,
    )
    back = exchange(big, order)
    token = shape(rows * width, blocks, dtype=BF16)
    out, gate_grad, value_grad, filt_grad = call(
        lambda *refs: unpack_kernel(width, *refs),
        (token, token, token, shape(rows, blocks, dtype=BF16)),
        back, gate, cotangent,
        limit=10 * MIB,
        scratch_shapes=[wide, wide],
    )
    return from_rows(out), from_rows(gate_grad), from_rows(value_grad), filt_grad


def solution(mesh):
    return jax.shard_map(
        per_device,
        mesh=mesh,
        in_specs=(P("seq", "ch", None), P("seq", "ch", None), P("seq", None), P("seq", "ch", None)),
        out_specs=(
            P("seq", "ch", None),
            P("seq", "ch", None),
            P("seq", "ch", None),
            P("seq", "ch"),
        ),
        check_vma=False,
    )
```

```python
import math

import jax
import jax.numpy as jnp
import numpy as np
from jax import lax
from jax.experimental import pallas as pl
from jax.experimental.pallas import tpu as pltpu
from jax.sharding import PartitionSpec as P

F32 = jnp.float32
BF16 = jnp.bfloat16
VMEM = pl.BlockSpec(memory_space=pltpu.VMEM)
HBM = pl.BlockSpec(memory_space=pltpu.HBM)
MIB = 1024 * 1024
STRIDE = 19


def two_parts(table):
    high = table.astype(jnp.bfloat16)
    low = (table - high.astype(np.float64)).astype(jnp.bfloat16)
    return high, low


def make_tables(rows, blocks, order):
    kappa = np.arange(blocks)[:, None]
    block = np.arange(blocks)[None, :]
    angle = math.pi / (2 * blocks) * ((2 * kappa + 1) * block % (4 * blocks))
    stage1 = np.concatenate([np.cos(angle), -np.sin(angle)], axis=0)
    row = np.arange(rows)[None, :]
    turn = math.pi / (2 * rows * blocks) * ((2 * kappa + 1) * row % (4 * rows * blocks))
    k = np.arange(rows)[None, :]
    angle = 2 * math.pi / rows * (np.arange(rows)[:, None] * k % rows)
    cos, sin = np.cos(angle), np.sin(angle)
    stage2 = np.concatenate(
        [np.concatenate([cos, -sin], axis=1), np.concatenate([sin, cos], axis=1)], axis=0
    )
    stage1 = stage1[:, order]
    back1 = stage1.T / (rows * blocks)
    back2 = stage2.T
    pieces = [np.concatenate(two_parts(stage1), axis=1)]
    for table in (stage2, back2, back1):
        pieces.extend(two_parts(table))
    pieces.extend(two_parts(np.concatenate([np.cos(turn), np.sin(turn)], axis=1)))
    return np.concatenate(pieces, axis=0)


class Tables:
    def __init__(self, table_ref):
        full = table_ref.shape[1]
        blocks = full // 2

        def rows(first, count, lanes=full):
            return table_ref[pl.ds(first, count), pl.ds(0, lanes)]

        self.blocks = blocks
        self.pair = lambda: rows(0, full)
        self.stage1_high = lambda: rows(0, full, blocks)
        self.stage2 = lambda: (rows(full, full), rows(2 * full, full))
        self.back2 = lambda: (rows(3 * full, full), rows(4 * full, full))
        self.back1 = lambda: (rows(5 * full, blocks), rows(5 * full + blocks, blocks))
        turn = rows(6 * full, blocks).astype(F32) + rows(6 * full + blocks, blocks).astype(F32)
        self.cos, self.sin = turn[:, :blocks], turn[:, blocks:]


def split(x):
    high = x.astype(BF16)
    return high, (x - high.astype(F32)).astype(BF16)


def dot(a, b):
    return jnp.dot(a, b, preferred_element_type=F32)


def left_dot(high, low, x):
    x_high, x_low = split(x)
    return dot(high, x_high) + dot(high, x_low) + dot(low, x_high)


def right_dot(x, high, low):
    x_high, x_low = split(x)
    return dot(x_high, high) + dot(x_low, high) + dot(x_high, low)


def lanes(x, index, width=128):
    return x[:, index * width:(index + 1) * width]


def transform(x_ref, firsts, stride, exact, tables):
    blocks, tc, ts = tables.blocks, tables.cos, tables.sin
    count = len(firsts)
    columns = [x_ref[pl.ds(first, blocks, stride=stride), :] for first in firsts]
    x = jnp.concatenate(columns, axis=1)
    if exact:
        x = x.astype(BF16)
        a = dot(tables.pair(), jnp.concatenate([x, x], axis=0))
    else:
        x, low = split(x)
        a = dot(tables.pair(), jnp.concatenate([x, x], axis=0)) + dot(tables.stage1_high(), low)
    re, im = a[:blocks], a[blocks:]
    pieces = []
    for c in range(count):
        cr, ci = lanes(re, c), lanes(im, c)
        pieces.append(
            jnp.concatenate([cr * tc + ci * ts, ci * tc - cr * ts], axis=1)
        )
    return right_dot(jnp.concatenate(pieces, axis=0), *tables.stage2())


def inverse(spectra, tables):
    blocks, tc, ts = tables.blocks, tables.cos, tables.sin
    count = spectra.shape[0] // blocks
    c = right_dot(spectra, *tables.back2())
    pieces = []
    for i in range(count):
        part = c[i * blocks:(i + 1) * blocks]
        cr, ci = lanes(part, 0), lanes(part, 1)
        pieces.append(
            jnp.concatenate([cr * tc - ci * ts, cr * ts + ci * tc], axis=0)
        )
    return left_dot(*tables.back1(), jnp.concatenate(pieces, axis=1))


def pack_kernel(
    width, parts, gate_hbm, value_hbm, cot_hbm, filt_hbm, out_ref,
    gate_ref, value_ref, cot_ref, filt_ref, v_ref, g_ref, sems,
):
    pairs = ((value_hbm, value_ref), (gate_hbm, gate_ref), (cot_hbm, cot_ref), (filt_hbm, filt_ref))
    copies = [pltpu.make_async_copy(a, b, sems.at[i]) for i, (a, b) in enumerate(pairs)]
    for copy in copies:
        copy.start()
    rows = filt_ref.shape[0]
    stride = out_ref.shape[0] // rows
    scale = 1.0 / math.sqrt(rows * rows)
    copies[0].wait()
    v_ref[...] = value_ref[...].astype(F32)
    for c in range(width):
        out_ref[pl.ds(c, rows, stride=stride), :] = v_ref[pl.ds(c, rows, stride=width), :].T
    copies[1].wait()
    copies[2].wait()
    g_ref[...] = cot_ref[...].astype(F32) * gate_ref[...].astype(F32)
    for c in range(width):
        out_ref[pl.ds(width + c, rows, stride=stride), :] = g_ref[pl.ds(c, rows, stride=width), :].T
    copies[3].wait()
    for c in range(parts):
        out_ref[pl.ds(2 * width + c, rows, stride=stride), :] = (
            lanes(filt_ref, c).astype(F32) * scale
        ).T


def correlation(vs_ref, gs_ref, firsts, blocks):
    total_re = total_im = 0.0
    for first in firsts:
        v, g = vs_ref[pl.ds(first, blocks), :], gs_ref[pl.ds(first, blocks), :]
        vr, vi, gr, gi = lanes(v, 0), lanes(v, 1), lanes(g, 0), lanes(g, 1)
        total_re += gr * vr + gi * vi
        total_im += gi * vr - gr * vi
    return jnp.concatenate([total_re, total_im], axis=1)


def others_kernel(group, parts, scale, x_ref, table_ref, dh_ref, vs_ref, gs_ref):
    tables = Tables(table_ref)
    blocks = tables.blocks
    stride = x_ref.shape[0] // blocks
    width = group * parts
    me = lax.axis_index("ch")
    others = [lax.rem(me + k, parts) for k in range(1, parts)]
    columns = [q * group + s for q in others for s in range(group)]
    vs_ref[...] = transform(x_ref, columns, stride, True, tables)
    gs_ref[...] = transform(x_ref, [width + c for c in columns], stride, False, tables)
    pieces = [
        correlation(vs_ref, gs_ref, [(i * group + s) * blocks for s in range(group)], blocks)
        for i in range(parts - 1)
    ]
    dh = inverse(jnp.concatenate(pieces, axis=0), tables)
    for i, q in enumerate(others):
        dh_ref[q] = lanes(dh, i) * scale
    dh_ref[me] = jnp.zeros_like(dh_ref[me])


def products_kernel(group, parts, scale, x_ref, table_ref, out_ref, vs_ref, gs_ref):
    tables = Tables(table_ref)
    blocks = tables.blocks
    stride = out_ref.shape[0] // blocks
    width = group * parts
    held = x_ref.shape[0] // blocks
    spectra = transform(x_ref, [2 * width + q for q in range(parts)], held, True, tables)
    for which, ref in enumerate((vs_ref, gs_ref)):
        columns = [which * width + c for c in range(width)]
        ref[...] = transform(x_ref, columns, held, which == 0, tables)
        sign = 1.0 if which == 0 else -1.0
        pieces = []
        for c in range(width):
            x = ref[pl.ds(c * blocks, blocks), :]
            q = c // group
            h = spectra[q * blocks:(q + 1) * blocks]
            xr, xi, hr, hi = lanes(x, 0), lanes(x, 1), lanes(h, 0), lanes(h, 1) * sign
            pieces.append(jnp.concatenate([xr * hr - xi * hi, xr * hi + xi * hr], axis=1))
        y = inverse(jnp.concatenate(pieces, axis=0), tables)
        for c in range(width):
            out_ref[pl.ds(which * width + c, blocks, stride=stride), :] = lanes(y, c)
    me = lax.axis_index("ch")
    own = [pl.multiple_of((me * group + s) * blocks, blocks) for s in range(group)]
    dh = inverse(correlation(vs_ref, gs_ref, own, blocks), tables)
    out_ref[pl.ds(2 * width, blocks, stride=stride), :] = dh * scale


def merge_kernel(dh_hbm, big_ref, out_ref, dh_ref, sems):
    parts, blocks, rows = dh_hbm.shape
    copies = [pltpu.make_async_copy(dh_hbm.at[q], dh_ref.at[q], sems.at[q]) for q in range(parts)]
    for copy in copies:
        copy.start()
    stride = out_ref.shape[0] // blocks
    out_ref[...] = big_ref[...]
    last = pl.ds(stride - 1, blocks, stride=stride)
    total = big_ref[last, :]
    for q in range(parts):
        copies[q].wait()
        total += dh_ref[q]
    out_ref[last, :] = total


def unpack_kernel(
    width, x_ref, gate_ref, cot_ref, out_hbm, gate_grad_hbm, value_grad_hbm, filt_hbm,
    conv_ref, grad_ref, out_ref, gate_grad_ref, value_grad_ref, filt_ref, sems,
):
    pairs = (
        (out_ref, out_hbm),
        (gate_grad_ref, gate_grad_hbm),
        (value_grad_ref, value_grad_hbm),
        (filt_ref, filt_hbm),
    )
    copies = [pltpu.make_async_copy(a, b, sems.at[i]) for i, (a, b) in enumerate(pairs)]
    rows = filt_ref.shape[0]
    stride = x_ref.shape[0] // rows
    for c in range(width):
        conv_ref[pl.ds(c, rows, stride=width), :] = x_ref[pl.ds(c, rows, stride=stride), :].T
    conv = conv_ref[...]
    out_ref[...] = (gate_ref[...].astype(F32) * conv).astype(BF16)
    copies[0].start()
    gate_grad_ref[...] = (cot_ref[...].astype(F32) * conv).astype(BF16)
    copies[1].start()
    for c in range(width):
        grad_ref[pl.ds(c, rows, stride=width), :] = x_ref[pl.ds(width + c, rows, stride=stride), :].T
    value_grad_ref[...] = grad_ref[...].astype(BF16)
    copies[2].start()
    filt_ref[...] = x_ref[pl.ds(2 * width, rows, stride=stride), :].T.astype(BF16)
    copies[3].start()
    for copy in copies:
        copy.wait()


def call(body, outs, *args, spaces=None, out_space=VMEM, limit=24 * MIB, **kw):
    return pl.pallas_call(
        body,
        out_shape=outs,
        in_specs=spaces or [VMEM] * len(args),
        out_specs=jax.tree.map(lambda _: out_space, outs),
        compiler_params=pltpu.CompilerParams(vmem_limit_bytes=limit),
        **kw,
    )(*args)


def in_hbm(x):
    return pltpu.with_memory_space_constraint(x, pltpu.HBM)


def exchange(x, order):
    flat = x.reshape(len(order), -1)
    out = lax.all_to_all(
        flat, "seq", split_axis=0, concat_axis=0, axis_index_groups=[order], tiled=True
    )
    return out.reshape(x.shape)


def per_device(gate, value, filt, cotangent):
    rows, group, filters = value.shape
    blocks = lax.axis_size("seq")
    parts = filters // blocks
    width = group * parts
    order = [STRIDE * i % blocks for i in range(blocks)]
    tables = make_tables(rows, blocks, order)

    def to_rows(x):
        x = x.reshape(rows, group, parts, blocks).transpose(0, 2, 1, 3)
        return x.reshape(rows * width, blocks)

    def from_rows(x):
        x = x.reshape(rows, parts, group, blocks).transpose(0, 2, 1, 3)
        return x.reshape(rows, group, filters)

    def shape(*dims, dtype=F32):
        return jax.ShapeDtypeStruct(dims, dtype)

    gate, value, cotangent = to_rows(gate), to_rows(value), to_rows(cotangent)
    wide = pltpu.VMEM((rows * width, blocks), F32)
    sent = call(
        lambda *refs: pack_kernel(width, parts, *refs),
        shape(blocks * (2 * width + parts), rows),
        *[in_hbm(x) for x in (gate, value, cotangent, filt)],
        spaces=[HBM] * 4,
        limit=24 * MIB,
        scratch_shapes=[
            *[pltpu.VMEM((rows * width, blocks), BF16)] * 3,
            pltpu.VMEM((rows, filters), BF16),
            wide,
            wide,
            pltpu.SemaphoreType.DMA((4,)),
        ],
    )
    held = exchange(sent, order)
    scale = 1.0 / math.sqrt(rows * blocks)
    some = pltpu.VMEM(((parts - 1) * group * blocks, 2 * rows), F32)
    dh = call(
        lambda *refs: others_kernel(group, parts, scale, *refs),
        shape(parts, blocks, rows),
        held, tables,
        scratch_shapes=[some, some],
    )
    dh = lax.all_to_all(dh, "ch", split_axis=0, concat_axis=0, tiled=True)
    spectra = pltpu.VMEM((width * blocks, 2 * rows), F32)
    big = call(
        lambda *refs: products_kernel(group, parts, scale, *refs),
        shape(blocks * (2 * width + 1), rows),
        held, tables,
        scratch_shapes=[spectra, spectra],
    )
    big = call(
        merge_kernel,
        shape(blocks * (2 * width + 1), rows),
        in_hbm(dh), big,
        spaces=[HBM, VMEM],
        limit=6 * MIB,
        scratch_shapes=[
            pltpu.VMEM((parts, blocks, rows), F32),
            pltpu.SemaphoreType.DMA((parts,)),
        ],
    )
    back = exchange(big, order)
    token = shape(rows * width, blocks, dtype=BF16)
    out, gate_grad, value_grad, filt_grad = call(
        lambda *refs: unpack_kernel(width, *refs),
        (token, token, token, shape(rows, blocks, dtype=BF16)),
        back, gate, cotangent,
        out_space=HBM,
        limit=10 * MIB,
        scratch_shapes=[
            wide,
            wide,
            *[pltpu.VMEM((rows * width, blocks), BF16)] * 3,
            pltpu.VMEM((rows, blocks), BF16),
            pltpu.SemaphoreType.DMA((4,)),
        ],
    )
    return from_rows(out), from_rows(gate_grad), from_rows(value_grad), filt_grad


def solution(mesh):
    return jax.shard_map(
        per_device,
        mesh=mesh,
        in_specs=(P("seq", "ch", None), P("seq", "ch", None), P("seq", None), P("seq", "ch", None)),
        out_specs=(
            P("seq", "ch", None),
            P("seq", "ch", None),
            P("seq", "ch", None),
            P("seq", "ch"),
        ),
        check_vma=False,
    )
```

```python
import math

import jax
import jax.numpy as jnp
import numpy as np
from jax import lax
from jax.experimental import pallas as pl
from jax.experimental.pallas import tpu as pltpu
from jax.sharding import PartitionSpec as P

F32 = jnp.float32
BF16 = jnp.bfloat16
VMEM = pl.BlockSpec(memory_space=pltpu.VMEM)
HBM = pl.BlockSpec(memory_space=pltpu.HBM)
MIB = 1024 * 1024
STRIDE = 19
LATE = 1


def two_parts(table):
    high = table.astype(jnp.bfloat16)
    low = (table - high.astype(np.float64)).astype(jnp.bfloat16)
    return high, low


def make_tables(rows, blocks, order):
    kappa = np.arange(blocks)[:, None]
    block = np.arange(blocks)[None, :]
    angle = math.pi / (2 * blocks) * ((2 * kappa + 1) * block % (4 * blocks))
    stage1 = np.concatenate([np.cos(angle), -np.sin(angle)], axis=0)
    row = np.arange(rows)[None, :]
    turn = math.pi / (2 * rows * blocks) * ((2 * kappa + 1) * row % (4 * rows * blocks))
    k = np.arange(rows)[None, :]
    angle = 2 * math.pi / rows * (np.arange(rows)[:, None] * k % rows)
    cos, sin = np.cos(angle), np.sin(angle)
    stage2 = np.concatenate(
        [np.concatenate([cos, -sin], axis=1), np.concatenate([sin, cos], axis=1)], axis=0
    )
    stage1 = stage1[:, order]
    back1 = stage1.T / (rows * blocks)
    back2 = stage2.T
    pieces = [np.concatenate(two_parts(stage1), axis=1)]
    for table in (stage2, back2, back1):
        pieces.extend(two_parts(table))
    pieces.extend(two_parts(np.concatenate([np.cos(turn), np.sin(turn)], axis=1)))
    return np.concatenate(pieces, axis=0)


class Tables:
    def __init__(self, table_ref):
        full = table_ref.shape[1]
        blocks = full // 2

        def rows(first, count, lanes=full):
            return table_ref[pl.ds(first, count), pl.ds(0, lanes)]

        self.blocks = blocks
        self.pair = lambda: rows(0, full)
        self.stage1_high = lambda: rows(0, full, blocks)
        self.stage2 = lambda: (rows(full, full), rows(2 * full, full))
        self.back2 = lambda: (rows(3 * full, full), rows(4 * full, full))
        self.back1 = lambda: (rows(5 * full, blocks), rows(5 * full + blocks, blocks))
        turn = rows(6 * full, blocks).astype(F32) + rows(6 * full + blocks, blocks).astype(F32)
        self.cos, self.sin = turn[:, :blocks], turn[:, blocks:]


def split(x):
    high = x.astype(BF16)
    return high, (x - high.astype(F32)).astype(BF16)


def dot(a, b):
    return jnp.dot(a, b, preferred_element_type=F32)


def left_dot(high, low, x):
    x_high, x_low = split(x)
    table = jnp.concatenate([high, high, low], axis=1)
    return dot(table, jnp.concatenate([x_high, x_low, x_high], axis=0))


def right_dot(x, high, low):
    x_high, x_low = split(x)
    table = jnp.concatenate([high, high, low], axis=0)
    return dot(jnp.concatenate([x_high, x_low, x_high], axis=1), table)


def lanes(x, index, width=128):
    return x[:, index * width:(index + 1) * width]


def transform(x_ref, firsts, stride, exact, tables):
    blocks, tc, ts = tables.blocks, tables.cos, tables.sin
    count = len(firsts)
    columns = [x_ref[pl.ds(first, blocks, stride=stride), :] for first in firsts]
    x = jnp.concatenate(columns, axis=1)
    if exact:
        x = x.astype(BF16)
        a = dot(tables.pair(), jnp.concatenate([x, x], axis=0))
    else:
        x, low = split(x)
        a = dot(tables.pair(), jnp.concatenate([x, x], axis=0)) + dot(tables.stage1_high(), low)
    re, im = a[:blocks], a[blocks:]
    pieces = []
    for c in range(count):
        cr, ci = lanes(re, c), lanes(im, c)
        pieces.append(
            jnp.concatenate([cr * tc + ci * ts, ci * tc - cr * ts], axis=1)
        )
    return right_dot(jnp.concatenate(pieces, axis=0), *tables.stage2())


def inverse(spectra, tables):
    blocks, tc, ts = tables.blocks, tables.cos, tables.sin
    count = spectra.shape[0] // blocks
    c = right_dot(spectra, *tables.back2())
    pieces = []
    for i in range(count):
        part = c[i * blocks:(i + 1) * blocks]
        cr, ci = lanes(part, 0), lanes(part, 1)
        pieces.append(
            jnp.concatenate([cr * tc - ci * ts, cr * ts + ci * tc], axis=0)
        )
    return left_dot(*tables.back1(), jnp.concatenate(pieces, axis=1))


def pack_kernel(
    width, parts, gate_hbm, value_hbm, cot_hbm, filt_hbm, out_ref,
    gate_ref, value_ref, cot_ref, filt_ref, v_ref, g_ref, sems,
):
    pairs = ((value_hbm, value_ref), (gate_hbm, gate_ref), (cot_hbm, cot_ref), (filt_hbm, filt_ref))
    copies = [pltpu.make_async_copy(a, b, sems.at[i]) for i, (a, b) in enumerate(pairs)]
    for copy in copies:
        copy.start()
    rows = filt_ref.shape[0]
    stride = out_ref.shape[0] // rows
    scale = 1.0 / math.sqrt(rows * rows)
    copies[0].wait()
    v_ref[...] = value_ref[...].astype(F32)
    for c in range(width):
        out_ref[pl.ds(c, rows, stride=stride), :] = v_ref[pl.ds(c, rows, stride=width), :].T
    copies[1].wait()
    copies[2].wait()
    g_ref[...] = cot_ref[...].astype(F32) * gate_ref[...].astype(F32)
    for c in range(width):
        out_ref[pl.ds(width + c, rows, stride=stride), :] = g_ref[pl.ds(c, rows, stride=width), :].T
    copies[3].wait()
    for c in range(parts):
        out_ref[pl.ds(2 * width + c, rows, stride=stride), :] = (
            lanes(filt_ref, c).astype(F32) * scale
        ).T


def correlation(vs_ref, gs_ref, firsts, blocks):
    total_re = total_im = 0.0
    for first in firsts:
        v, g = vs_ref[pl.ds(first, blocks), :], gs_ref[pl.ds(first, blocks), :]
        vr, vi, gr, gi = lanes(v, 0), lanes(v, 1), lanes(g, 0), lanes(g, 1)
        total_re += gr * vr + gi * vi
        total_im += gi * vr - gr * vi
    return jnp.concatenate([total_re, total_im], axis=1)


def others_kernel(group, parts, scale, x_ref, table_ref, dh_ref, vs_ref, gs_ref):
    tables = Tables(table_ref)
    blocks = tables.blocks
    stride = x_ref.shape[0] // blocks
    width = group * parts
    me = lax.axis_index("ch")
    others = [lax.rem(me + k, parts) for k in range(1, parts)]
    columns = [q * group + s for q in others for s in range(group)]
    vs_ref[...] = transform(x_ref, columns, stride, True, tables)
    gs_ref[...] = transform(x_ref, [width + c for c in columns], stride, False, tables)
    pieces = [
        correlation(vs_ref, gs_ref, [(i * group + s) * blocks for s in range(group)], blocks)
        for i in range(parts - 1)
    ]
    dh = inverse(jnp.concatenate(pieces, axis=0), tables)
    for i, q in enumerate(others):
        dh_ref[q] = lanes(dh, i) * scale
    dh_ref[me] = jnp.zeros_like(dh_ref[me])


def products_kernel(group, parts, scale, x_ref, table_ref, out_ref, vs_ref, gs_ref):
    tables = Tables(table_ref)
    blocks = tables.blocks
    width = group * parts
    stride = 2 * width + 1
    late = (out_ref.shape[0] // blocks - stride) // 2
    held = x_ref.shape[0] // blocks
    spectra = transform(x_ref, [2 * width + q for q in range(parts)], held, True, tables)
    for which, ref in enumerate((vs_ref, gs_ref)):
        columns = [which * width + c for c in range(width)]
        ref[...] = transform(x_ref, columns, held, which == 0, tables)
        sign = 1.0 if which == 0 else -1.0
        pieces = []
        for c in range(width):
            x = ref[pl.ds(c * blocks, blocks), :]
            q = c // group
            h = spectra[q * blocks:(q + 1) * blocks]
            xr, xi, hr, hi = lanes(x, 0), lanes(x, 1), lanes(h, 0), lanes(h, 1) * sign
            pieces.append(jnp.concatenate([xr * hr - xi * hi, xr * hi + xi * hr], axis=1))
        here = width if which == 0 else width - late
        y = inverse(jnp.concatenate(pieces[:here], axis=0), tables)
        for c in range(here):
            out_ref[pl.ds(which * width + c, blocks, stride=stride), :] = lanes(y, c)
        if here < width:
            rest = jnp.concatenate(pieces[here:], axis=0)
            for half in range(2):
                at = pl.ds((stride + half * late) * blocks, late * blocks)
                out_ref[at, :] = lanes(rest, half)
    me = lax.axis_index("ch")
    own = [pl.multiple_of((me * group + s) * blocks, blocks) for s in range(group)]
    dh = inverse(correlation(vs_ref, gs_ref, own, blocks), tables)
    out_ref[pl.ds(2 * width, blocks, stride=stride), :] = dh * scale


def merge_kernel(dh_hbm, big_ref, table_ref, out_ref, dh_ref, sems):
    parts, blocks, rows = dh_hbm.shape
    copies = [pltpu.make_async_copy(dh_hbm.at[q], dh_ref.at[q], sems.at[q]) for q in range(parts)]
    for copy in copies:
        copy.start()
    stride = out_ref.shape[0] // blocks
    out_ref[...] = big_ref[pl.ds(0, stride * blocks), :]
    late = (big_ref.shape[0] // blocks - stride) // 2
    rest = [
        big_ref[pl.ds((stride + half * late) * blocks, late * blocks), :] for half in range(2)
    ]
    y = inverse(jnp.concatenate(rest, axis=1), Tables(table_ref))
    for c in range(late):
        out_ref[pl.ds(stride - 1 - late + c, blocks, stride=stride), :] = lanes(y, c)
    last = pl.ds(stride - 1, blocks, stride=stride)
    total = big_ref[last, :]
    for q in range(parts):
        copies[q].wait()
        total += dh_ref[q]
    out_ref[last, :] = total


def unpack_kernel(
    width, x_ref, gate_ref, cot_ref, out_hbm, gate_grad_hbm, value_grad_hbm, filt_hbm,
    conv_ref, grad_ref, out_ref, gate_grad_ref, value_grad_ref, filt_ref, sems,
):
    pairs = (
        (out_ref, out_hbm),
        (gate_grad_ref, gate_grad_hbm),
        (value_grad_ref, value_grad_hbm),
        (filt_ref, filt_hbm),
    )
    copies = [pltpu.make_async_copy(a, b, sems.at[i]) for i, (a, b) in enumerate(pairs)]
    rows = filt_ref.shape[0]
    stride = x_ref.shape[0] // rows
    for c in range(width):
        conv_ref[pl.ds(c, rows, stride=width), :] = x_ref[pl.ds(c, rows, stride=stride), :].T
    conv = conv_ref[...]
    out_ref[...] = (gate_ref[...].astype(F32) * conv).astype(BF16)
    copies[0].start()
    gate_grad_ref[...] = (cot_ref[...].astype(F32) * conv).astype(BF16)
    copies[1].start()
    for c in range(width):
        grad_ref[pl.ds(c, rows, stride=width), :] = x_ref[pl.ds(width + c, rows, stride=stride), :].T
    value_grad_ref[...] = grad_ref[...].astype(BF16)
    copies[2].start()
    filt_ref[...] = x_ref[pl.ds(2 * width, rows, stride=stride), :].T.astype(BF16)
    copies[3].start()
    for copy in copies:
        copy.wait()


def call(body, outs, *args, spaces=None, out_space=VMEM, limit=24 * MIB, **kw):
    return pl.pallas_call(
        body,
        out_shape=outs,
        in_specs=spaces or [VMEM] * len(args),
        out_specs=jax.tree.map(lambda _: out_space, outs),
        compiler_params=pltpu.CompilerParams(vmem_limit_bytes=limit),
        **kw,
    )(*args)


def in_hbm(x):
    return pltpu.with_memory_space_constraint(x, pltpu.HBM)


def exchange(x, order):
    flat = x.reshape(len(order), -1)
    out = lax.all_to_all(
        flat, "seq", split_axis=0, concat_axis=0, axis_index_groups=[order], tiled=True
    )
    return out.reshape(x.shape)


def per_device(gate, value, filt, cotangent):
    rows, group, filters = value.shape
    blocks = lax.axis_size("seq")
    parts = filters // blocks
    width = group * parts
    order = [STRIDE * i % blocks for i in range(blocks)]
    tables = make_tables(rows, blocks, order)

    def to_rows(x):
        x = x.reshape(rows, group, parts, blocks).transpose(0, 2, 1, 3)
        return x.reshape(rows * width, blocks)

    def from_rows(x):
        x = x.reshape(rows, parts, group, blocks).transpose(0, 2, 1, 3)
        return x.reshape(rows, group, filters)

    def shape(*dims, dtype=F32):
        return jax.ShapeDtypeStruct(dims, dtype)

    gate, value, cotangent = to_rows(gate), to_rows(value), to_rows(cotangent)
    wide = pltpu.VMEM((rows * width, blocks), F32)
    sent = call(
        lambda *refs: pack_kernel(width, parts, *refs),
        shape(blocks * (2 * width + parts), rows),
        *[in_hbm(x) for x in (gate, value, cotangent, filt)],
        spaces=[HBM] * 4,
        limit=24 * MIB,
        scratch_shapes=[
            *[pltpu.VMEM((rows * width, blocks), BF16)] * 3,
            pltpu.VMEM((rows, filters), BF16),
            wide,
            wide,
            pltpu.SemaphoreType.DMA((4,)),
        ],
    )
    held = exchange(sent, order)
    scale = 1.0 / math.sqrt(rows * blocks)
    some = pltpu.VMEM(((parts - 1) * group * blocks, 2 * rows), F32)
    dh = call(
        lambda *refs: others_kernel(group, parts, scale, *refs),
        shape(parts, blocks, rows),
        held, tables,
        scratch_shapes=[some, some],
    )
    dh = lax.all_to_all(dh, "ch", split_axis=0, concat_axis=0, tiled=True)
    spectra = pltpu.VMEM((width * blocks, 2 * rows), F32)
    big = call(
        lambda *refs: products_kernel(group, parts, scale, *refs),
        shape(blocks * (2 * width + 1 + 2 * LATE), rows),
        held, tables,
        scratch_shapes=[spectra, spectra],
    )
    big = call(
        merge_kernel,
        shape(blocks * (2 * width + 1), rows),
        in_hbm(dh), big, tables,
        spaces=[HBM, VMEM, VMEM],
        limit=12 * MIB,
        scratch_shapes=[
            pltpu.VMEM((parts, blocks, rows), F32),
            pltpu.SemaphoreType.DMA((parts,)),
        ],
    )
    back = exchange(big, order)
    token = shape(rows * width, blocks, dtype=BF16)
    out, gate_grad, value_grad, filt_grad = call(
        lambda *refs: unpack_kernel(width, *refs),
        (token, token, token, shape(rows, blocks, dtype=BF16)),
        back, gate, cotangent,
        out_space=HBM,
        limit=10 * MIB,
        scratch_shapes=[
            wide,
            wide,
            *[pltpu.VMEM((rows * width, blocks), BF16)] * 3,
            pltpu.VMEM((rows, blocks), BF16),
            pltpu.SemaphoreType.DMA((4,)),
        ],
    )
    return from_rows(out), from_rows(gate_grad), from_rows(value_grad), filt_grad


def solution(mesh):
    return jax.shard_map(
        per_device,
        mesh=mesh,
        in_specs=(P("seq", "ch", None), P("seq", "ch", None), P("seq", None), P("seq", "ch", None)),
        out_specs=(
            P("seq", "ch", None),
            P("seq", "ch", None),
            P("seq", "ch", None),
            P("seq", "ch"),
        ),
        check_vma=False,
    )
```

```python
import math

import jax
import jax.numpy as jnp
import numpy as np
from jax import lax
from jax.experimental import pallas as pl
from jax.experimental.pallas import tpu as pltpu
from jax.sharding import PartitionSpec as P

F32 = jnp.float32
BF16 = jnp.bfloat16
VMEM = pl.BlockSpec(memory_space=pltpu.VMEM)
HBM = pl.BlockSpec(memory_space=pltpu.HBM)
MIB = 1024 * 1024
STRIDE = 1
LATE = 1


def two_parts(table):
    high = table.astype(jnp.bfloat16)
    low = (table - high.astype(np.float64)).astype(jnp.bfloat16)
    return high, low


def make_tables(rows, blocks, order):
    kappa = np.arange(blocks)[:, None]
    block = np.arange(blocks)[None, :]
    angle = math.pi / (2 * blocks) * ((2 * kappa + 1) * block % (4 * blocks))
    stage1 = np.concatenate([np.cos(angle), -np.sin(angle)], axis=0)
    row = np.arange(rows)[None, :]
    turn = math.pi / (2 * rows * blocks) * ((2 * kappa + 1) * row % (4 * rows * blocks))
    k = np.arange(rows)[None, :]
    angle = 2 * math.pi / rows * (np.arange(rows)[:, None] * k % rows)
    cos, sin = np.cos(angle), np.sin(angle)
    stage2 = np.concatenate(
        [np.concatenate([cos, -sin], axis=1), np.concatenate([sin, cos], axis=1)], axis=0
    )
    stage1 = stage1[:, order]
    back1 = stage1.T / (rows * blocks)
    back2 = stage2.T
    pieces = [np.concatenate(two_parts(stage1), axis=1)]
    for table in (stage2, back2, back1):
        pieces.extend(two_parts(table))
    pieces.extend(two_parts(np.concatenate([np.cos(turn), np.sin(turn)], axis=1)))
    return np.concatenate(pieces, axis=0)


class Tables:
    def __init__(self, table_ref):
        full = table_ref.shape[1]
        blocks = full // 2

        def rows(first, count, lanes=full):
            return table_ref[pl.ds(first, count), pl.ds(0, lanes)]

        self.blocks = blocks
        self.pair = lambda: rows(0, full)
        self.stage1_high = lambda: rows(0, full, blocks)
        self.stage2 = lambda: (rows(full, full), rows(2 * full, full))
        self.back2 = lambda: (rows(3 * full, full), rows(4 * full, full))
        self.back1 = lambda: (rows(5 * full, blocks), rows(5 * full + blocks, blocks))
        turn = rows(6 * full, blocks).astype(F32) + rows(6 * full + blocks, blocks).astype(F32)
        self.cos, self.sin = turn[:, :blocks], turn[:, blocks:]


def split(x):
    high = x.astype(BF16)
    return high, (x - high.astype(F32)).astype(BF16)


def dot(a, b):
    return jnp.dot(a, b, preferred_element_type=F32)


def left_dot(high, low, x):
    x_high, x_low = split(x)
    table = jnp.concatenate([high, high, low], axis=1)
    return dot(table, jnp.concatenate([x_high, x_low, x_high], axis=0))


def right_dot(x, high, low):
    x_high, x_low = split(x)
    table = jnp.concatenate([high, high, low], axis=0)
    return dot(jnp.concatenate([x_high, x_low, x_high], axis=1), table)


def lanes(x, index, width=128):
    return x[:, index * width:(index + 1) * width]


def transform(x_ref, firsts, stride, exact, tables):
    blocks, tc, ts = tables.blocks, tables.cos, tables.sin
    count = len(firsts)
    columns = [x_ref[pl.ds(first, blocks, stride=stride), :] for first in firsts]
    x = jnp.concatenate(columns, axis=1)
    if exact:
        x = x.astype(BF16)
        a = dot(tables.pair(), jnp.concatenate([x, x], axis=0))
    else:
        x, low = split(x)
        a = dot(tables.pair(), jnp.concatenate([x, x], axis=0)) + dot(tables.stage1_high(), low)
    re, im = a[:blocks], a[blocks:]
    pieces = []
    for c in range(count):
        cr, ci = lanes(re, c), lanes(im, c)
        pieces.append(
            jnp.concatenate([cr * tc + ci * ts, ci * tc - cr * ts], axis=1)
        )
    return right_dot(jnp.concatenate(pieces, axis=0), *tables.stage2())


def inverse(spectra, tables):
    blocks, tc, ts = tables.blocks, tables.cos, tables.sin
    count = spectra.shape[0] // blocks
    c = right_dot(spectra, *tables.back2())
    pieces = []
    for i in range(count):
        part = c[i * blocks:(i + 1) * blocks]
        cr, ci = lanes(part, 0), lanes(part, 1)
        pieces.append(
            jnp.concatenate([cr * tc - ci * ts, cr * ts + ci * tc], axis=0)
        )
    return left_dot(*tables.back1(), jnp.concatenate(pieces, axis=1))


def pack_kernel(
    width, parts, gate_hbm, value_hbm, cot_hbm, filt_hbm, out_ref,
    gate_ref, value_ref, cot_ref, filt_ref, v_ref, g_ref, sems,
):
    pairs = ((value_hbm, value_ref), (gate_hbm, gate_ref), (cot_hbm, cot_ref), (filt_hbm, filt_ref))
    copies = [pltpu.make_async_copy(a, b, sems.at[i]) for i, (a, b) in enumerate(pairs)]
    for copy in copies:
        copy.start()
    rows = filt_ref.shape[0]
    stride = out_ref.shape[0] // rows
    scale = 1.0 / math.sqrt(rows * rows)
    copies[0].wait()
    v_ref[...] = value_ref[...].astype(F32)
    for c in range(width):
        out_ref[pl.ds(c, rows, stride=stride), :] = v_ref[pl.ds(c, rows, stride=width), :].T
    copies[1].wait()
    copies[2].wait()
    g_ref[...] = cot_ref[...].astype(F32) * gate_ref[...].astype(F32)
    for c in range(width):
        out_ref[pl.ds(width + c, rows, stride=stride), :] = g_ref[pl.ds(c, rows, stride=width), :].T
    copies[3].wait()
    for c in range(parts):
        out_ref[pl.ds(2 * width + c, rows, stride=stride), :] = (
            lanes(filt_ref, c).astype(F32) * scale
        ).T


def correlation(vs_ref, gs_ref, firsts, blocks):
    total_re = total_im = 0.0
    for first in firsts:
        v, g = vs_ref[pl.ds(first, blocks), :], gs_ref[pl.ds(first, blocks), :]
        vr, vi, gr, gi = lanes(v, 0), lanes(v, 1), lanes(g, 0), lanes(g, 1)
        total_re += gr * vr + gi * vi
        total_im += gi * vr - gr * vi
    return jnp.concatenate([total_re, total_im], axis=1)


def others_kernel(group, parts, scale, x_ref, table_ref, dh_ref, vs_ref, gs_ref):
    tables = Tables(table_ref)
    blocks = tables.blocks
    stride = x_ref.shape[0] // blocks
    width = group * parts
    me = lax.axis_index("ch")
    others = [lax.rem(me + k, parts) for k in range(1, parts)]
    columns = [q * group + s for q in others for s in range(group)]
    vs_ref[...] = transform(x_ref, columns, stride, True, tables)
    gs_ref[...] = transform(x_ref, [width + c for c in columns], stride, False, tables)
    pieces = [
        correlation(vs_ref, gs_ref, [(i * group + s) * blocks for s in range(group)], blocks)
        for i in range(parts - 1)
    ]
    dh = inverse(jnp.concatenate(pieces, axis=0), tables)
    for i, q in enumerate(others):
        dh_ref[q] = lanes(dh, i) * scale
    dh_ref[me] = jnp.zeros_like(dh_ref[me])


def products_kernel(group, parts, scale, x_ref, table_ref, out_ref, vs_ref, gs_ref):
    tables = Tables(table_ref)
    blocks = tables.blocks
    width = group * parts
    stride = 2 * width + 1
    late = (out_ref.shape[0] // blocks - stride) // 2
    held = x_ref.shape[0] // blocks
    spectra = transform(x_ref, [2 * width + q for q in range(parts)], held, True, tables)
    for which, ref in enumerate((vs_ref, gs_ref)):
        columns = [which * width + c for c in range(width)]
        ref[...] = transform(x_ref, columns, held, which == 0, tables)
        sign = 1.0 if which == 0 else -1.0
        pieces = []
        for c in range(width):
            x = ref[pl.ds(c * blocks, blocks), :]
            q = c // group
            h = spectra[q * blocks:(q + 1) * blocks]
            xr, xi, hr, hi = lanes(x, 0), lanes(x, 1), lanes(h, 0), lanes(h, 1) * sign
            pieces.append(jnp.concatenate([xr * hr - xi * hi, xr * hi + xi * hr], axis=1))
        here = width if which == 0 else width - late
        y = inverse(jnp.concatenate(pieces[:here], axis=0), tables)
        for c in range(here):
            out_ref[pl.ds(which * width + c, blocks, stride=stride), :] = lanes(y, c)
        if here < width:
            rest = jnp.concatenate(pieces[here:], axis=0)
            for half in range(2):
                at = pl.ds((stride + half * late) * blocks, late * blocks)
                out_ref[at, :] = lanes(rest, half)
    me = lax.axis_index("ch")
    own = [pl.multiple_of((me * group + s) * blocks, blocks) for s in range(group)]
    dh = inverse(correlation(vs_ref, gs_ref, own, blocks), tables)
    out_ref[pl.ds(2 * width, blocks, stride=stride), :] = dh * scale


def merge_kernel(dh_hbm, big_ref, table_ref, out_ref, dh_ref, sems):
    parts, blocks, rows = dh_hbm.shape
    copies = [pltpu.make_async_copy(dh_hbm.at[q], dh_ref.at[q], sems.at[q]) for q in range(parts)]
    for copy in copies:
        copy.start()
    stride = out_ref.shape[0] // blocks
    out_ref[...] = big_ref[pl.ds(0, stride * blocks), :]
    late = (big_ref.shape[0] // blocks - stride) // 2
    rest = [
        big_ref[pl.ds((stride + half * late) * blocks, late * blocks), :] for half in range(2)
    ]
    y = inverse(jnp.concatenate(rest, axis=1), Tables(table_ref))
    for c in range(late):
        out_ref[pl.ds(stride - 1 - late + c, blocks, stride=stride), :] = lanes(y, c)
    last = pl.ds(stride - 1, blocks, stride=stride)
    total = big_ref[last, :]
    for q in range(parts):
        copies[q].wait()
        total += dh_ref[q]
    out_ref[last, :] = total


def unpack_kernel(
    width, x_ref, gate_ref, cot_ref, out_hbm, gate_grad_hbm, value_grad_hbm, filt_hbm,
    conv_ref, grad_ref, out_ref, gate_grad_ref, value_grad_ref, filt_ref, sems,
):
    pairs = (
        (out_ref, out_hbm),
        (gate_grad_ref, gate_grad_hbm),
        (value_grad_ref, value_grad_hbm),
        (filt_ref, filt_hbm),
    )
    copies = [pltpu.make_async_copy(a, b, sems.at[i]) for i, (a, b) in enumerate(pairs)]
    rows = filt_ref.shape[0]
    stride = x_ref.shape[0] // rows
    for c in range(width):
        conv_ref[pl.ds(c, rows, stride=width), :] = x_ref[pl.ds(c, rows, stride=stride), :].T
    conv = conv_ref[...]
    out_ref[...] = (gate_ref[...].astype(F32) * conv).astype(BF16)
    copies[0].start()
    gate_grad_ref[...] = (cot_ref[...].astype(F32) * conv).astype(BF16)
    copies[1].start()
    for c in range(width):
        grad_ref[pl.ds(c, rows, stride=width), :] = x_ref[pl.ds(width + c, rows, stride=stride), :].T
    value_grad_ref[...] = grad_ref[...].astype(BF16)
    copies[2].start()
    filt_ref[...] = x_ref[pl.ds(2 * width, rows, stride=stride), :].T.astype(BF16)
    copies[3].start()
    for copy in copies:
        copy.wait()


def call(body, outs, *args, spaces=None, out_space=VMEM, limit=24 * MIB, **kw):
    return pl.pallas_call(
        body,
        out_shape=outs,
        in_specs=spaces or [VMEM] * len(args),
        out_specs=jax.tree.map(lambda _: out_space, outs),
        compiler_params=pltpu.CompilerParams(vmem_limit_bytes=limit),
        **kw,
    )(*args)


def in_hbm(x):
    return pltpu.with_memory_space_constraint(x, pltpu.HBM)


def exchange(x, order):
    flat = x.reshape(len(order), -1)
    out = lax.all_to_all(
        flat, "seq", split_axis=0, concat_axis=0, axis_index_groups=[order], tiled=True
    )
    return out.reshape(x.shape)


def per_device(gate, value, filt, cotangent):
    rows, group, filters = value.shape
    blocks = lax.axis_size("seq")
    parts = filters // blocks
    width = group * parts
    order = [STRIDE * i % blocks for i in range(blocks)]
    tables = make_tables(rows, blocks, order)

    def to_rows(x):
        x = x.reshape(rows, group, parts, blocks).transpose(0, 2, 1, 3)
        return x.reshape(rows * width, blocks)

    def from_rows(x):
        x = x.reshape(rows, parts, group, blocks).transpose(0, 2, 1, 3)
        return x.reshape(rows, group, filters)

    def shape(*dims, dtype=F32):
        return jax.ShapeDtypeStruct(dims, dtype)

    gate, value, cotangent = to_rows(gate), to_rows(value), to_rows(cotangent)
    wide = pltpu.VMEM((rows * width, blocks), F32)
    sent = call(
        lambda *refs: pack_kernel(width, parts, *refs),
        shape(blocks * (2 * width + parts), rows),
        *[in_hbm(x) for x in (gate, value, cotangent, filt)],
        spaces=[HBM] * 4,
        limit=24 * MIB,
        scratch_shapes=[
            *[pltpu.VMEM((rows * width, blocks), BF16)] * 3,
            pltpu.VMEM((rows, filters), BF16),
            wide,
            wide,
            pltpu.SemaphoreType.DMA((4,)),
        ],
    )
    held = exchange(sent, order)
    scale = 1.0 / math.sqrt(rows * blocks)
    some = pltpu.VMEM(((parts - 1) * group * blocks, 2 * rows), F32)
    dh = call(
        lambda *refs: others_kernel(group, parts, scale, *refs),
        shape(parts, blocks, rows),
        held, tables,
        scratch_shapes=[some, some],
    )
    dh = lax.all_to_all(dh, "ch", split_axis=0, concat_axis=0, tiled=True)
    spectra = pltpu.VMEM((width * blocks, 2 * rows), F32)
    big = call(
        lambda *refs: products_kernel(group, parts, scale, *refs),
        shape(blocks * (2 * width + 1 + 2 * LATE), rows),
        held, tables,
        scratch_shapes=[spectra, spectra],
    )
    big = call(
        merge_kernel,
        shape(blocks * (2 * width + 1), rows),
        in_hbm(dh), big, tables,
        spaces=[HBM, VMEM, VMEM],
        limit=12 * MIB,
        scratch_shapes=[
            pltpu.VMEM((parts, blocks, rows), F32),
            pltpu.SemaphoreType.DMA((parts,)),
        ],
    )
    back = exchange(big, order)
    token = shape(rows * width, blocks, dtype=BF16)
    out, gate_grad, value_grad, filt_grad = call(
        lambda *refs: unpack_kernel(width, *refs),
        (token, token, token, shape(rows, blocks, dtype=BF16)),
        back, gate, cotangent,
        out_space=HBM,
        limit=10 * MIB,
        scratch_shapes=[
            wide,
            wide,
            *[pltpu.VMEM((rows * width, blocks), BF16)] * 3,
            pltpu.VMEM((rows, blocks), BF16),
            pltpu.SemaphoreType.DMA((4,)),
        ],
    )
    return from_rows(out), from_rows(gate_grad), from_rows(value_grad), filt_grad


def solution(mesh):
    return jax.shard_map(
        per_device,
        mesh=mesh,
        in_specs=(P("seq", "ch", None), P("seq", "ch", None), P("seq", None), P("seq", "ch", None)),
        out_specs=(
            P("seq", "ch", None),
            P("seq", "ch", None),
            P("seq", "ch", None),
            P("seq", "ch"),
        ),
        check_vma=False,
    )
```

```python
import math

import jax
import jax.numpy as jnp
import numpy as np
from jax import lax
from jax.experimental import pallas as pl
from jax.experimental.pallas import tpu as pltpu
from jax.sharding import PartitionSpec as P

F32 = jnp.float32
BF16 = jnp.bfloat16
VMEM = pl.BlockSpec(memory_space=pltpu.VMEM)
HBM = pl.BlockSpec(memory_space=pltpu.HBM)
MIB = 1024 * 1024
LATE = 1


def two_parts(table):
    high = table.astype(jnp.bfloat16)
    low = (table - high.astype(np.float64)).astype(jnp.bfloat16)
    return high, low


def make_tables(rows, blocks, order):
    kappa = np.arange(blocks)[:, None]
    block = np.arange(blocks)[None, :]
    angle = math.pi / (2 * blocks) * ((2 * kappa + 1) * block % (4 * blocks))
    stage1 = np.concatenate([np.cos(angle), -np.sin(angle)], axis=0)
    row = np.arange(rows)[None, :]
    turn = math.pi / (2 * rows * blocks) * ((2 * kappa + 1) * row % (4 * rows * blocks))
    k = np.arange(rows)[None, :]
    angle = 2 * math.pi / rows * (np.arange(rows)[:, None] * k % rows)
    cos, sin = np.cos(angle), np.sin(angle)
    stage2 = np.concatenate(
        [np.concatenate([cos, -sin], axis=1), np.concatenate([sin, cos], axis=1)], axis=0
    )
    stage1 = stage1[:, order]
    back1 = stage1.T / (rows * blocks)
    back2 = stage2.T
    pieces = [np.concatenate(two_parts(stage1), axis=1)]
    for table in (stage2, back2, back1):
        pieces.extend(two_parts(table))
    pieces.extend(two_parts(np.concatenate([np.cos(turn), np.sin(turn)], axis=1)))
    return np.concatenate(pieces, axis=0)


class Tables:
    def __init__(self, table_ref):
        full = table_ref.shape[1]
        blocks = full // 2

        def rows(first, count, lanes=full):
            return table_ref[pl.ds(first, count), pl.ds(0, lanes)]

        self.blocks = blocks
        self.pair = lambda: rows(0, full)
        self.stage1_high = lambda: rows(0, full, blocks)
        self.stage2 = lambda: (rows(full, full), rows(2 * full, full))
        self.back2 = lambda: (rows(3 * full, full), rows(4 * full, full))
        self.back1 = lambda: (rows(5 * full, blocks), rows(5 * full + blocks, blocks))
        turn = rows(6 * full, blocks).astype(F32) + rows(6 * full + blocks, blocks).astype(F32)
        self.cos, self.sin = turn[:, :blocks], turn[:, blocks:]


def split(x):
    high = x.astype(BF16)
    return high, (x - high.astype(F32)).astype(BF16)


def dot(a, b):
    return jnp.dot(a, b, preferred_element_type=F32)


def left_dot(high, low, x):
    x_high, x_low = split(x)
    table = jnp.concatenate([high, high, low], axis=1)
    return dot(table, jnp.concatenate([x_high, x_low, x_high], axis=0))


def right_dot(x, high, low):
    x_high, x_low = split(x)
    table = jnp.concatenate([high, high, low], axis=0)
    return dot(jnp.concatenate([x_high, x_low, x_high], axis=1), table)


def lanes(x, index, width=128):
    return x[:, index * width:(index + 1) * width]


def transform(x_ref, firsts, stride, exact, tables):
    blocks, tc, ts = tables.blocks, tables.cos, tables.sin
    count = len(firsts)
    columns = [x_ref[pl.ds(first, blocks, stride=stride), :] for first in firsts]
    x = jnp.concatenate(columns, axis=1)
    if exact:
        x = x.astype(BF16)
        a = dot(tables.pair(), jnp.concatenate([x, x], axis=0))
    else:
        x, low = split(x)
        a = dot(tables.pair(), jnp.concatenate([x, x], axis=0)) + dot(tables.stage1_high(), low)
    re, im = a[:blocks], a[blocks:]
    pieces = []
    for c in range(count):
        cr, ci = lanes(re, c), lanes(im, c)
        pieces.append(
            jnp.concatenate([cr * tc + ci * ts, ci * tc - cr * ts], axis=1)
        )
    return right_dot(jnp.concatenate(pieces, axis=0), *tables.stage2())


def inverse(spectra, tables):
    blocks, tc, ts = tables.blocks, tables.cos, tables.sin
    count = spectra.shape[0] // blocks
    c = right_dot(spectra, *tables.back2())
    pieces = []
    for i in range(count):
        part = c[i * blocks:(i + 1) * blocks]
        cr, ci = lanes(part, 0), lanes(part, 1)
        pieces.append(
            jnp.concatenate([cr * tc - ci * ts, cr * ts + ci * tc], axis=0)
        )
    return left_dot(*tables.back1(), jnp.concatenate(pieces, axis=1))


def pack_kernel(
    width, parts, gate_hbm, value_hbm, cot_hbm, filt_hbm, out_ref,
    gate_ref, value_ref, cot_ref, filt_ref, v_ref, g_ref, sems,
):
    pairs = ((value_hbm, value_ref), (gate_hbm, gate_ref), (cot_hbm, cot_ref), (filt_hbm, filt_ref))
    copies = [pltpu.make_async_copy(a, b, sems.at[i]) for i, (a, b) in enumerate(pairs)]
    for copy in copies:
        copy.start()
    rows = filt_ref.shape[0]
    stride = out_ref.shape[0] // rows
    scale = 1.0 / math.sqrt(rows * rows)
    copies[0].wait()
    v_ref[...] = value_ref[...].astype(F32)
    for c in range(width):
        out_ref[pl.ds(c, rows, stride=stride), :] = v_ref[pl.ds(c, rows, stride=width), :].T
    copies[1].wait()
    copies[2].wait()
    g_ref[...] = cot_ref[...].astype(F32) * gate_ref[...].astype(F32)
    for c in range(width):
        out_ref[pl.ds(width + c, rows, stride=stride), :] = g_ref[pl.ds(c, rows, stride=width), :].T
    copies[3].wait()
    for c in range(parts):
        out_ref[pl.ds(2 * width + c, rows, stride=stride), :] = (
            lanes(filt_ref, c).astype(F32) * scale
        ).T


def correlation(vs_ref, gs_ref, firsts, blocks):
    total_re = total_im = 0.0
    for first in firsts:
        v, g = vs_ref[pl.ds(first, blocks), :], gs_ref[pl.ds(first, blocks), :]
        vr, vi, gr, gi = lanes(v, 0), lanes(v, 1), lanes(g, 0), lanes(g, 1)
        total_re += gr * vr + gi * vi
        total_im += gi * vr - gr * vi
    return jnp.concatenate([total_re, total_im], axis=1)


def others_kernel(group, parts, scale, x_ref, table_ref, dh_ref, vs_ref, gs_ref):
    tables = Tables(table_ref)
    blocks = tables.blocks
    stride = x_ref.shape[0] // blocks
    width = group * parts
    me = lax.axis_index("ch")
    others = [lax.rem(me + k, parts) for k in range(1, parts)]
    columns = [q * group + s for q in others for s in range(group)]
    vs_ref[...] = transform(x_ref, columns, stride, True, tables)
    gs_ref[...] = transform(x_ref, [width + c for c in columns], stride, False, tables)
    pieces = [
        correlation(vs_ref, gs_ref, [(i * group + s) * blocks for s in range(group)], blocks)
        for i in range(parts - 1)
    ]
    dh = inverse(jnp.concatenate(pieces, axis=0), tables)
    for i, q in enumerate(others):
        dh_ref[q] = lanes(dh, i) * scale
    dh_ref[me] = jnp.zeros_like(dh_ref[me])


def products_kernel(group, parts, scale, x_ref, table_ref, out_ref, vs_ref, gs_ref):
    tables = Tables(table_ref)
    blocks = tables.blocks
    width = group * parts
    stride = 2 * width + 1
    late = (out_ref.shape[0] // blocks - stride) // 2
    held = x_ref.shape[0] // blocks
    spectra = transform(x_ref, [2 * width + q for q in range(parts)], held, True, tables)
    for which, ref in enumerate((vs_ref, gs_ref)):
        columns = [which * width + c for c in range(width)]
        ref[...] = transform(x_ref, columns, held, which == 0, tables)
        sign = 1.0 if which == 0 else -1.0
        pieces = []
        for c in range(width):
            x = ref[pl.ds(c * blocks, blocks), :]
            q = c // group
            h = spectra[q * blocks:(q + 1) * blocks]
            xr, xi, hr, hi = lanes(x, 0), lanes(x, 1), lanes(h, 0), lanes(h, 1) * sign
            pieces.append(jnp.concatenate([xr * hr - xi * hi, xr * hi + xi * hr], axis=1))
        here = width if which == 0 else width - late
        y = inverse(jnp.concatenate(pieces[:here], axis=0), tables)
        for c in range(here):
            out_ref[pl.ds(which * width + c, blocks, stride=stride), :] = lanes(y, c)
        if here < width:
            rest = jnp.concatenate(pieces[here:], axis=0)
            for half in range(2):
                at = pl.ds((stride + half * late) * blocks, late * blocks)
                out_ref[at, :] = lanes(rest, half)
    me = lax.axis_index("ch")
    own = [pl.multiple_of((me * group + s) * blocks, blocks) for s in range(group)]
    dh = inverse(correlation(vs_ref, gs_ref, own, blocks), tables)
    out_ref[pl.ds(2 * width, blocks, stride=stride), :] = dh * scale


def merge_kernel(dh_hbm, big_ref, table_ref, out_ref, dh_ref, sems):
    parts, blocks, rows = dh_hbm.shape
    copies = [pltpu.make_async_copy(dh_hbm.at[q], dh_ref.at[q], sems.at[q]) for q in range(parts)]
    for copy in copies:
        copy.start()
    stride = out_ref.shape[0] // blocks
    out_ref[...] = big_ref[pl.ds(0, stride * blocks), :]
    late = (big_ref.shape[0] // blocks - stride) // 2
    rest = [
        big_ref[pl.ds((stride + half * late) * blocks, late * blocks), :] for half in range(2)
    ]
    y = inverse(jnp.concatenate(rest, axis=1), Tables(table_ref))
    for c in range(late):
        out_ref[pl.ds(stride - 1 - late + c, blocks, stride=stride), :] = lanes(y, c)
    last = pl.ds(stride - 1, blocks, stride=stride)
    total = big_ref[last, :]
    for q in range(parts):
        copies[q].wait()
        total += dh_ref[q]
    out_ref[last, :] = total


def unpack_kernel(
    width, x_ref, gate_ref, cot_ref, out_hbm, gate_grad_hbm, value_grad_hbm, filt_hbm,
    conv_ref, grad_ref, out_ref, gate_grad_ref, value_grad_ref, filt_ref, sems,
):
    pairs = (
        (out_ref, out_hbm),
        (gate_grad_ref, gate_grad_hbm),
        (value_grad_ref, value_grad_hbm),
        (filt_ref, filt_hbm),
    )
    copies = [pltpu.make_async_copy(a, b, sems.at[i]) for i, (a, b) in enumerate(pairs)]
    rows = filt_ref.shape[0]
    stride = x_ref.shape[0] // rows
    for c in range(width):
        conv_ref[pl.ds(c, rows, stride=width), :] = x_ref[pl.ds(c, rows, stride=stride), :].T
    conv = conv_ref[...]
    out_ref[...] = (gate_ref[...].astype(F32) * conv).astype(BF16)
    copies[0].start()
    gate_grad_ref[...] = (cot_ref[...].astype(F32) * conv).astype(BF16)
    copies[1].start()
    for c in range(width):
        grad_ref[pl.ds(c, rows, stride=width), :] = x_ref[pl.ds(width + c, rows, stride=stride), :].T
    value_grad_ref[...] = grad_ref[...].astype(BF16)
    copies[2].start()
    filt_ref[...] = x_ref[pl.ds(2 * width, rows, stride=stride), :].T.astype(BF16)
    copies[3].start()
    for copy in copies:
        copy.wait()


def call(body, outs, *args, spaces=None, out_space=VMEM, limit=24 * MIB, **kw):
    return pl.pallas_call(
        body,
        out_shape=outs,
        in_specs=spaces or [VMEM] * len(args),
        out_specs=jax.tree.map(lambda _: out_space, outs),
        compiler_params=pltpu.CompilerParams(vmem_limit_bytes=limit),
        **kw,
    )(*args)


def in_hbm(x):
    return pltpu.with_memory_space_constraint(x, pltpu.HBM)


def exchange(x, order):
    flat = x.reshape(len(order), -1)
    out = lax.all_to_all(
        flat, "seq", split_axis=0, concat_axis=0, axis_index_groups=[order], tiled=True
    )
    return out.reshape(x.shape)


def per_device(gate, value, filt, cotangent):
    rows, group, filters = value.shape
    blocks = lax.axis_size("seq")
    parts = filters // blocks
    width = group * parts
    side = math.isqrt(blocks // 2)
    grid = np.arange(blocks).reshape(blocks // (2 * side), side, 2)
    order = [int(i) for i in grid.transpose(1, 0, 2).reshape(-1)]
    tables = make_tables(rows, blocks, order)

    def to_rows(x):
        x = x.reshape(rows, group, parts, blocks).transpose(0, 2, 1, 3)
        return x.reshape(rows * width, blocks)

    def from_rows(x):
        x = x.reshape(rows, parts, group, blocks).transpose(0, 2, 1, 3)
        return x.reshape(rows, group, filters)

    def shape(*dims, dtype=F32):
        return jax.ShapeDtypeStruct(dims, dtype)

    gate, value, cotangent = to_rows(gate), to_rows(value), to_rows(cotangent)
    wide = pltpu.VMEM((rows * width, blocks), F32)
    sent = call(
        lambda *refs: pack_kernel(width, parts, *refs),
        shape(blocks * (2 * width + parts), rows),
        *[in_hbm(x) for x in (gate, value, cotangent, filt)],
        spaces=[HBM] * 4,
        limit=24 * MIB,
        scratch_shapes=[
            *[pltpu.VMEM((rows * width, blocks), BF16)] * 3,
            pltpu.VMEM((rows, filters), BF16),
            wide,
            wide,
            pltpu.SemaphoreType.DMA((4,)),
        ],
    )
    held = exchange(sent, order)
    scale = 1.0 / math.sqrt(rows * blocks)
    some = pltpu.VMEM(((parts - 1) * group * blocks, 2 * rows), F32)
    dh = call(
        lambda *refs: others_kernel(group, parts, scale, *refs),
        shape(parts, blocks, rows),
        held, tables,
        scratch_shapes=[some, some],
    )
    dh = lax.all_to_all(dh, "ch", split_axis=0, concat_axis=0, tiled=True)
    spectra = pltpu.VMEM((width * blocks, 2 * rows), F32)
    big = call(
        lambda *refs: products_kernel(group, parts, scale, *refs),
        shape(blocks * (2 * width + 1 + 2 * LATE), rows),
        held, tables,
        scratch_shapes=[spectra, spectra],
    )
    big = call(
        merge_kernel,
        shape(blocks * (2 * width + 1), rows),
        in_hbm(dh), big, tables,
        spaces=[HBM, VMEM, VMEM],
        limit=12 * MIB,
        scratch_shapes=[
            pltpu.VMEM((parts, blocks, rows), F32),
            pltpu.SemaphoreType.DMA((parts,)),
        ],
    )
    back = exchange(big, order)
    token = shape(rows * width, blocks, dtype=BF16)
    out, gate_grad, value_grad, filt_grad = call(
        lambda *refs: unpack_kernel(width, *refs),
        (token, token, token, shape(rows, blocks, dtype=BF16)),
        back, gate, cotangent,
        out_space=HBM,
        limit=10 * MIB,
        scratch_shapes=[
            wide,
            wide,
            *[pltpu.VMEM((rows * width, blocks), BF16)] * 3,
            pltpu.VMEM((rows, blocks), BF16),
            pltpu.SemaphoreType.DMA((4,)),
        ],
    )
    return from_rows(out), from_rows(gate_grad), from_rows(value_grad), filt_grad


def solution(mesh):
    return jax.shard_map(
        per_device,
        mesh=mesh,
        in_specs=(P("seq", "ch", None), P("seq", "ch", None), P("seq", None), P("seq", "ch", None)),
        out_specs=(
            P("seq", "ch", None),
            P("seq", "ch", None),
            P("seq", "ch", None),
            P("seq", "ch"),
        ),
        check_vma=False,
    )
```

```python
import math

import jax
import jax.numpy as jnp
import numpy as np
from jax import lax
from jax.experimental import pallas as pl
from jax.experimental.pallas import tpu as pltpu
from jax.sharding import PartitionSpec as P

F32 = jnp.float32
BF16 = jnp.bfloat16
VMEM = pl.BlockSpec(memory_space=pltpu.VMEM)
HBM = pl.BlockSpec(memory_space=pltpu.HBM)
MIB = 1024 * 1024
LATE = 1


def two_parts(table):
    high = table.astype(jnp.bfloat16)
    low = (table - high.astype(np.float64)).astype(jnp.bfloat16)
    return high, low


def make_tables(rows, blocks, order):
    kappa = np.arange(blocks)[:, None]
    block = np.arange(blocks)[None, :]
    angle = math.pi / (2 * blocks) * ((2 * kappa + 1) * block % (4 * blocks))
    stage1 = np.concatenate([np.cos(angle), -np.sin(angle)], axis=0)
    row = np.arange(rows)[None, :]
    turn = math.pi / (2 * rows * blocks) * ((2 * kappa + 1) * row % (4 * rows * blocks))
    k = np.arange(rows)[None, :]
    angle = 2 * math.pi / rows * (np.arange(rows)[:, None] * k % rows)
    cos, sin = np.cos(angle), np.sin(angle)
    stage2 = np.concatenate(
        [np.concatenate([cos, -sin], axis=1), np.concatenate([sin, cos], axis=1)], axis=0
    )
    stage1 = stage1[:, order]
    back1 = stage1.T / (rows * blocks)
    back2 = stage2.T
    pieces = [np.concatenate(two_parts(stage1), axis=1)]
    for table in (stage2, back2, back1):
        pieces.extend(two_parts(table))
    pieces.extend(two_parts(np.concatenate([np.cos(turn), np.sin(turn)], axis=1)))
    return np.concatenate(pieces, axis=0)


class Tables:
    def __init__(self, table_ref):
        full = table_ref.shape[1]
        blocks = full // 2

        def rows(first, count, lanes=full):
            return table_ref[pl.ds(first, count), pl.ds(0, lanes)]

        self.blocks = blocks
        self.pair = lambda: rows(0, full)
        self.stage1_high = lambda: rows(0, full, blocks)
        self.stage2 = lambda: (rows(full, full), rows(2 * full, full))
        self.back2 = lambda: (rows(3 * full, full), rows(4 * full, full))
        self.back1 = lambda: (rows(5 * full, blocks), rows(5 * full + blocks, blocks))
        turn = rows(6 * full, blocks).astype(F32) + rows(6 * full + blocks, blocks).astype(F32)
        self.cos, self.sin = turn[:, :blocks], turn[:, blocks:]


def split(x):
    high = x.astype(BF16)
    return high, (x - high.astype(F32)).astype(BF16)


def dot(a, b):
    return jnp.dot(a, b, preferred_element_type=F32)


def left_dot(high, low, x):
    x_high, x_low = split(x)
    table = jnp.concatenate([high, high, low], axis=1)
    return dot(table, jnp.concatenate([x_high, x_low, x_high], axis=0))


def right_dot(x, high, low):
    x_high, x_low = split(x)
    table = jnp.concatenate([high, high, low], axis=0)
    return dot(jnp.concatenate([x_high, x_low, x_high], axis=1), table)


def lanes(x, index, width=128):
    return x[:, index * width:(index + 1) * width]


def transform(x_ref, firsts, stride, exact, tables):
    blocks, tc, ts = tables.blocks, tables.cos, tables.sin
    count = len(firsts)
    columns = [x_ref[pl.ds(first, blocks, stride=stride), :] for first in firsts]
    x = jnp.concatenate(columns, axis=1)
    if exact:
        x = x.astype(BF16)
        a = dot(tables.pair(), jnp.concatenate([x, x], axis=0))
    else:
        x, low = split(x)
        a = dot(tables.pair(), jnp.concatenate([x, x], axis=0)) + dot(tables.stage1_high(), low)
    re, im = a[:blocks], a[blocks:]
    pieces = []
    for c in range(count):
        cr, ci = lanes(re, c), lanes(im, c)
        pieces.append(
            jnp.concatenate([cr * tc + ci * ts, ci * tc - cr * ts], axis=1)
        )
    return right_dot(jnp.concatenate(pieces, axis=0), *tables.stage2())


def inverse(spectra, tables):
    blocks, tc, ts = tables.blocks, tables.cos, tables.sin
    count = spectra.shape[0] // blocks
    c = right_dot(spectra, *tables.back2())
    pieces = []
    for i in range(count):
        part = c[i * blocks:(i + 1) * blocks]
        cr, ci = lanes(part, 0), lanes(part, 1)
        pieces.append(
            jnp.concatenate([cr * tc - ci * ts, cr * ts + ci * tc], axis=0)
        )
    return left_dot(*tables.back1(), jnp.concatenate(pieces, axis=1))


def pack_kernel(
    width, parts, gate_hbm, value_hbm, cot_hbm, filt_hbm, out_ref,
    gate_ref, value_ref, cot_ref, filt_ref, v_ref, g_ref, sems,
):
    pairs = ((value_hbm, value_ref), (gate_hbm, gate_ref), (cot_hbm, cot_ref), (filt_hbm, filt_ref))
    copies = [pltpu.make_async_copy(a, b, sems.at[i]) for i, (a, b) in enumerate(pairs)]
    for copy in copies:
        copy.start()
    rows = filt_ref.shape[0]
    stride = out_ref.shape[0] // rows
    scale = 1.0 / math.sqrt(rows * rows)
    copies[0].wait()
    v_ref[...] = value_ref[...].astype(F32)
    for c in range(width):
        out_ref[pl.ds(c, rows, stride=stride), :] = v_ref[pl.ds(c, rows, stride=width), :].T
    copies[1].wait()
    copies[2].wait()
    g_ref[...] = cot_ref[...].astype(F32) * gate_ref[...].astype(F32)
    for c in range(width):
        out_ref[pl.ds(width + c, rows, stride=stride), :] = g_ref[pl.ds(c, rows, stride=width), :].T
    copies[3].wait()
    for c in range(parts):
        out_ref[pl.ds(2 * width + c, rows, stride=stride), :] = (
            lanes(filt_ref, c).astype(F32) * scale
        ).T


def correlation(vs_ref, gs_ref, firsts, blocks):
    total_re = total_im = 0.0
    for first in firsts:
        v, g = vs_ref[pl.ds(first, blocks), :], gs_ref[pl.ds(first, blocks), :]
        vr, vi, gr, gi = lanes(v, 0), lanes(v, 1), lanes(g, 0), lanes(g, 1)
        total_re += gr * vr + gi * vi
        total_im += gi * vr - gr * vi
    return jnp.concatenate([total_re, total_im], axis=1)


def others_kernel(group, parts, scale, x_ref, table_ref, dh_ref, vs_ref, gs_ref):
    tables = Tables(table_ref)
    blocks = tables.blocks
    stride = x_ref.shape[0] // blocks
    width = group * parts
    me = lax.axis_index("ch")
    others = [lax.rem(me + k, parts) for k in range(1, parts)]
    columns = [q * group + s for q in others for s in range(group)]
    vs_ref[...] = transform(x_ref, columns, stride, True, tables)
    gs_ref[...] = transform(x_ref, [width + c for c in columns], stride, False, tables)
    pieces = [
        correlation(vs_ref, gs_ref, [(i * group + s) * blocks for s in range(group)], blocks)
        for i in range(parts - 1)
    ]
    dh = inverse(jnp.concatenate(pieces, axis=0), tables)
    for i, q in enumerate(others):
        dh_ref[q] = lanes(dh, i) * scale
    dh_ref[me] = jnp.zeros_like(dh_ref[me])


def products_kernel(group, parts, scale, x_ref, table_ref, out_ref, vs_ref, gs_ref):
    tables = Tables(table_ref)
    blocks = tables.blocks
    width = group * parts
    stride = 2 * width + 1
    late = (out_ref.shape[0] // blocks - stride) // 2
    held = x_ref.shape[0] // blocks
    spectra = transform(x_ref, [2 * width + q for q in range(parts)], held, True, tables)
    for which, ref in enumerate((vs_ref, gs_ref)):
        columns = [which * width + c for c in range(width)]
        ref[...] = transform(x_ref, columns, held, which == 0, tables)
        sign = 1.0 if which == 0 else -1.0
        pieces = []
        for c in range(width):
            x = ref[pl.ds(c * blocks, blocks), :]
            q = c // group
            h = spectra[q * blocks:(q + 1) * blocks]
            xr, xi, hr, hi = lanes(x, 0), lanes(x, 1), lanes(h, 0), lanes(h, 1) * sign
            pieces.append(jnp.concatenate([xr * hr - xi * hi, xr * hi + xi * hr], axis=1))
        here = width if which == 0 else width - late
        y = inverse(jnp.concatenate(pieces[:here], axis=0), tables)
        for c in range(here):
            out_ref[pl.ds(which * width + c, blocks, stride=stride), :] = lanes(y, c)
        if here < width:
            rest = jnp.concatenate(pieces[here:], axis=0)
            for half in range(2):
                at = pl.ds((stride + half * late) * blocks, late * blocks)
                out_ref[at, :] = lanes(rest, half)
    me = lax.axis_index("ch")
    own = [pl.multiple_of((me * group + s) * blocks, blocks) for s in range(group)]
    dh = inverse(correlation(vs_ref, gs_ref, own, blocks), tables)
    out_ref[pl.ds(2 * width, blocks, stride=stride), :] = dh * scale


def merge_kernel(dh_hbm, big_ref, table_ref, out_ref, dh_ref, sems):
    parts, blocks, rows = dh_hbm.shape
    copies = [pltpu.make_async_copy(dh_hbm.at[q], dh_ref.at[q], sems.at[q]) for q in range(parts)]
    for copy in copies:
        copy.start()
    stride = out_ref.shape[0] // blocks
    out_ref[...] = big_ref[pl.ds(0, stride * blocks), :]
    late = (big_ref.shape[0] // blocks - stride) // 2
    rest = [
        big_ref[pl.ds((stride + half * late) * blocks, late * blocks), :] for half in range(2)
    ]
    y = inverse(jnp.concatenate(rest, axis=1), Tables(table_ref))
    for c in range(late):
        out_ref[pl.ds(stride - 1 - late + c, blocks, stride=stride), :] = lanes(y, c)
    last = pl.ds(stride - 1, blocks, stride=stride)
    total = big_ref[last, :]
    for q in range(parts):
        copies[q].wait()
        total += dh_ref[q]
    out_ref[last, :] = total


def unpack_kernel(
    width, x_ref, gate_ref, cot_ref, out_hbm, gate_grad_hbm, value_grad_hbm, filt_hbm,
    conv_ref, grad_ref, out_ref, gate_grad_ref, value_grad_ref, filt_ref, sems,
):
    pairs = (
        (out_ref, out_hbm),
        (gate_grad_ref, gate_grad_hbm),
        (value_grad_ref, value_grad_hbm),
        (filt_ref, filt_hbm),
    )
    copies = [pltpu.make_async_copy(a, b, sems.at[i]) for i, (a, b) in enumerate(pairs)]
    rows = filt_ref.shape[0]
    stride = x_ref.shape[0] // rows
    for c in range(width):
        conv_ref[pl.ds(c, rows, stride=width), :] = x_ref[pl.ds(c, rows, stride=stride), :].T
    conv = conv_ref[...]
    out_ref[...] = (gate_ref[...].astype(F32) * conv).astype(BF16)
    copies[0].start()
    gate_grad_ref[...] = (cot_ref[...].astype(F32) * conv).astype(BF16)
    copies[1].start()
    for c in range(width):
        grad_ref[pl.ds(c, rows, stride=width), :] = x_ref[pl.ds(width + c, rows, stride=stride), :].T
    value_grad_ref[...] = grad_ref[...].astype(BF16)
    copies[2].start()
    filt_ref[...] = x_ref[pl.ds(2 * width, rows, stride=stride), :].T.astype(BF16)
    copies[3].start()
    for copy in copies:
        copy.wait()


def call(body, outs, *args, spaces=None, out_space=VMEM, limit=24 * MIB, **kw):
    return pl.pallas_call(
        body,
        out_shape=outs,
        in_specs=spaces or [VMEM] * len(args),
        out_specs=jax.tree.map(lambda _: out_space, outs),
        compiler_params=pltpu.CompilerParams(vmem_limit_bytes=limit),
        **kw,
    )(*args)


def in_hbm(x):
    return pltpu.with_memory_space_constraint(x, pltpu.HBM)


def exchange(x, order):
    flat = x.reshape(len(order), -1)
    out = lax.all_to_all(
        flat, "seq", split_axis=0, concat_axis=0, axis_index_groups=[order], tiled=True
    )
    return out.reshape(x.shape)


def per_device(gate, value, filt, cotangent):
    rows, group, filters = value.shape
    blocks = lax.axis_size("seq")
    parts = filters // blocks
    width = group * parts
    side = math.isqrt(blocks // 2)
    z, y, core = np.arange(blocks) // (2 * side), np.arange(blocks) // 2 % side, np.arange(blocks) % 2
    order = [int(i) for i in np.lexsort((y, core, (z - y) % side))]
    tables = make_tables(rows, blocks, order)

    def to_rows(x):
        x = x.reshape(rows, group, parts, blocks).transpose(0, 2, 1, 3)
        return x.reshape(rows * width, blocks)

    def from_rows(x):
        x = x.reshape(rows, parts, group, blocks).transpose(0, 2, 1, 3)
        return x.reshape(rows, group, filters)

    def shape(*dims, dtype=F32):
        return jax.ShapeDtypeStruct(dims, dtype)

    gate, value, cotangent = to_rows(gate), to_rows(value), to_rows(cotangent)
    wide = pltpu.VMEM((rows * width, blocks), F32)
    sent = call(
        lambda *refs: pack_kernel(width, parts, *refs),
        shape(blocks * (2 * width + parts), rows),
        *[in_hbm(x) for x in (gate, value, cotangent, filt)],
        spaces=[HBM] * 4,
        limit=24 * MIB,
        scratch_shapes=[
            *[pltpu.VMEM((rows * width, blocks), BF16)] * 3,
            pltpu.VMEM((rows, filters), BF16),
            wide,
            wide,
            pltpu.SemaphoreType.DMA((4,)),
        ],
    )
    held = exchange(sent, order)
    scale = 1.0 / math.sqrt(rows * blocks)
    some = pltpu.VMEM(((parts - 1) * group * blocks, 2 * rows), F32)
    dh = call(
        lambda *refs: others_kernel(group, parts, scale, *refs),
        shape(parts, blocks, rows),
        held, tables,
        scratch_shapes=[some, some],
    )
    dh = lax.all_to_all(dh, "ch", split_axis=0, concat_axis=0, tiled=True)
    spectra = pltpu.VMEM((width * blocks, 2 * rows), F32)
    big = call(
        lambda *refs: products_kernel(group, parts, scale, *refs),
        shape(blocks * (2 * width + 1 + 2 * LATE), rows),
        held, tables,
        scratch_shapes=[spectra, spectra],
    )
    big = call(
        merge_kernel,
        shape(blocks * (2 * width + 1), rows),
        in_hbm(dh), big, tables,
        spaces=[HBM, VMEM, VMEM],
        limit=12 * MIB,
        scratch_shapes=[
            pltpu.VMEM((parts, blocks, rows), F32),
            pltpu.SemaphoreType.DMA((parts,)),
        ],
    )
    back = exchange(big, order)
    token = shape(rows * width, blocks, dtype=BF16)
    out, gate_grad, value_grad, filt_grad = call(
        lambda *refs: unpack_kernel(width, *refs),
        (token, token, token, shape(rows, blocks, dtype=BF16)),
        back, gate, cotangent,
        out_space=HBM,
        limit=10 * MIB,
        scratch_shapes=[
            wide,
            wide,
            *[pltpu.VMEM((rows * width, blocks), BF16)] * 3,
            pltpu.VMEM((rows, blocks), BF16),
            pltpu.SemaphoreType.DMA((4,)),
        ],
    )
    return from_rows(out), from_rows(gate_grad), from_rows(value_grad), filt_grad


def solution(mesh):
    return jax.shard_map(
        per_device,
        mesh=mesh,
        in_specs=(P("seq", "ch", None), P("seq", "ch", None), P("seq", None), P("seq", "ch", None)),
        out_specs=(
            P("seq", "ch", None),
            P("seq", "ch", None),
            P("seq", "ch", None),
            P("seq", "ch"),
        ),
        check_vma=False,
    )
```
